256 devices in a mesh: gz: 8 (over x, core), yx: 32 (over y, z).
Axes of the slice: x: 4, y: 4, z: 8, core: 2. Of those that a mesh axis runs over, the one named last changes fastest.
Arguments:
- features: bfloat16 [16, 128, 512, 128], P(None, 'gz', 'yx'), may hold values from -19 to 19
- conv_weight: bfloat16 [3, 16, 3, 3, 3], replicated, may hold values from -0.3125 to 0.3125
- conv_bias: float32 [3], replicated, may hold values from -3 to 3
- labels: int32 [128, 512, 128], P('gz', 'yx'), may hold values from 0 to 8, as said below
Outputs:
- probabilities: float32 [8, 128, 512, 128], P(None, 'gz', 'yx')
- affinities: float32 [3, 128, 512, 128], P(None, 'gz', 'yx')
The draws below stay inside these ranges and needn't reach their ends.
Inputs may be any that keep to these rules, and one draw needn't show every extreme that they name: `labels`: 0 marks an unseeded voxel, k marks a seed of colour k.
All inputs are finite; a program needn't handle non-finite values.
Results may differ from the reference program's by a relative error of at most 0.0012.
Values may be sent and summed in bfloat16 or wider, within the bound.
A program may use at most 64 MiB of HBM per device.

```python
import jax
import jax.numpy as jnp
from jax import lax

CH = 16
FIELDS = 8
ITERS = 3
X = 128
NZ = 128
NY = 512


def draw_features(key, part):
    draw_shape = (CH, NZ, NY, X)
    depth_pos = jnp.arange(NZ, dtype=jnp.float32) / (NZ - 1)
    z_scale = (1.0 + 2.0 * depth_pos)[None, :, None, None]
    base_draw = jnp.clip(jax.random.normal(key, draw_shape, jnp.float32), -6.0, 6.0)
    values = base_draw * z_scale
    return values.astype(jnp.bfloat16)


def draw_labels(key, part):
    raw_values = jax.random.randint(key, (NZ, NY, X), 0, 64)
    colours = jnp.where(raw_values < 8, raw_values + 1, 0).astype(jnp.int32)
    return colours.at[0, 0, 0].set(8)


def noise(stream_key, shape, spread, limit, held_as=jnp.bfloat16):
    result = spread * jax.random.normal(stream_key, shape, jnp.float32)
    return jnp.clip(result, min=-limit, max=limit).astype(held_as)


def setup_inputs(seed: int = 0) -> dict:
    seeds = jax.random.split(jax.random.key(seed), 5)
    features = draw_features(jax.random.fold_in(seeds[4], 71), 0)
    conv_weight = noise(seeds[1], (3, CH, 3, 3, 3), (27 * CH) ** -0.5, 0.3125)
    conv_bias = noise(seeds[2], (3,), 1.0, 3.0, jnp.float32)
    labels = draw_labels(jax.random.fold_in(seeds[4], 71), 0)
    return {"features": features, "conv_weight": conv_weight, "conv_bias": conv_bias, "labels": labels}


RIDGE_WEIGHT = 0.5


def affinity_head(features, conv_weight, conv_bias):
    padded = jnp.pad(features, ((0, 0), (1, 1), (1, 1), (1, 1)))
    kernel = conv_weight.astype(jnp.float32)

    def plane_out(depth):
        slab_block = lax.dynamic_slice_in_dim(padded, depth, 3, 1).astype(jnp.float32)
        summed = jnp.zeros((3, NY, X), jnp.float32)
        for offset_z in range(3):
            for offset_y in range(3):
                for offset_x in range(3):
                    window = slab_block[:, offset_z, offset_y:offset_y + NY, offset_x:offset_x + X]
                    summed = summed + jnp.einsum("oc,cyx->oyx", kernel[:, :, offset_z, offset_y, offset_x], window, precision=lax.Precision.HIGHEST)
        return summed

    response = lax.map(plane_out, jnp.arange(NZ, dtype=jnp.int32))
    response = jnp.moveaxis(response, 0, 1)
    return jax.nn.sigmoid(response + conv_bias[:, None, None, None])


def edge_weights(affinities):
    keep_z = (jnp.arange(NZ, dtype=jnp.int32) < NZ - 1).astype(jnp.float32)[:, None, None]
    keep_y = (jnp.arange(NY, dtype=jnp.int32) < NY - 1).astype(jnp.float32)[None, :, None]
    keep_x = (jnp.arange(X, dtype=jnp.int32) < X - 1).astype(jnp.float32)[None, None, :]
    weight_zup = affinities[0] * keep_z
    weight_yup = affinities[1] * keep_y
    weight_xup = affinities[2] * keep_x
    weight_zdown = jnp.pad(weight_zup, ((1, 0), (0, 0), (0, 0)))[:-1]
    weight_ydown = jnp.pad(weight_yup, ((0, 0), (1, 0), (0, 0)))[:, :-1]
    weight_xdown = jnp.pad(weight_xup, ((0, 0), (0, 0), (1, 0)))[:, :, :-1]
    return weight_zup, weight_zdown, weight_yup, weight_ydown, weight_xup, weight_xdown


def operate(field, weights, seeded):
    weight_zup, weight_zdown, weight_yup, weight_ydown, weight_xup, weight_xdown = weights
    padded = jnp.pad(field, 1)
    laplace = weight_zup * (field - padded[2:, 1:-1, 1:-1]) + weight_zdown * (field - padded[:-2, 1:-1, 1:-1])
    laplace = laplace + weight_yup * (field - padded[1:-1, 2:, 1:-1]) + weight_ydown * (field - padded[1:-1, :-2, 1:-1])
    laplace = laplace + weight_xup * (field - padded[1:-1, 1:-1, 2:]) + weight_xdown * (field - padded[1:-1, 1:-1, :-2])
    return (1.0 - seeded) * (laplace + RIDGE_WEIGHT * field) + seeded * field


def reference(features, conv_weight, conv_bias, labels):
    affinities = affinity_head(features, conv_weight, conv_bias)
    weights = edge_weights(affinities)
    seeded = (labels > 0).astype(jnp.float32)

    def solve_field(label_index):
        seed_field = (labels == label_index + 1).astype(jnp.float32)
        right_side = seed_field - operate(seed_field, weights, seeded)
        solution = jnp.zeros_like(right_side)
        residual = right_side
        direction = right_side
        norm_now = jnp.sum(residual * residual)
        for iteration in range(ITERS):
            applied = operate(direction, weights, seeded)
            step_size = norm_now / jnp.sum(direction * applied)
            solution = solution + step_size * direction
            residual = residual - step_size * applied
            norm_next = jnp.sum(residual * residual)
            direction = residual + (norm_next / norm_now) * direction
            norm_now = norm_next
        return seed_field + solution

    probabilities = lax.map(solve_field, jnp.arange(FIELDS, dtype=jnp.int32))
    return probabilities, affinities
```

```python
import jax
import jax.numpy as jnp
from jax import lax
from jax.experimental import pallas as pl
from jax.experimental.pallas import tpu as pltpu
from jax.sharding import PartitionSpec as P

MESH = pl.DeviceIdType.MESH
FIELDS = 8
ITERS = 3
RIDGE = 0.5
N = 16
X = 128
CH = 16
LOW = 3
EXT = N + 7
ROWS = 4 * (N + 2)
F32 = jnp.float32

STEP_LOW, STEP_HIGH = 1.0 / 12.5, 2.0
BETA_HIGH = 25.0


def lane_iota(shape):
    return lax.broadcasted_iota(jnp.int32, shape, len(shape) - 1)


def row_iota(shape):
    return lax.broadcasted_iota(jnp.int32, shape, len(shape) - 2)


def spread_row(row):
    return jnp.broadcast_to(row, (8, X))


def build_weights(taps_ref, lhs_ref):
    columns = 3 * CH * N
    expand = (lax.div(lane_iota((3 * CH, columns)), N) == row_iota((3 * CH, columns))).astype(jnp.bfloat16)
    taps = jnp.dot(taps_ref[...], expand, preferred_element_type=F32)
    y_in = lax.rem(lane_iota((8, columns)), N)
    half = lax.div(row_iota((8, columns)), 4)
    for dx in range(3):
        for pair in range(0, (N + 2) // 2, 2):
            blocks = []
            for p in (pair, pair + 1):
                if p >= (N + 2) // 2:
                    continue
                gap = y_in - (2 * p - 1 + half) + 1
                block = jnp.zeros((8, columns), F32)
                for dy in range(3):
                    at = (dy * 3 + dx) * 8
                    block = jnp.where(gap == dy, taps[at : at + 8], block)
                blocks.append(block)
            at = dx * 80 + pair * 8
            if len(blocks) == 1:
                blocks.append(jnp.zeros((8, columns), F32))
            lhs_ref[at : at + 16, :] = jnp.concatenate(blocks, axis=0).astype(jnp.bfloat16)


def sigmoid(x):
    e = jnp.exp(-jnp.abs(x))
    s = 1.0 / (1.0 + e)
    return jnp.where(x >= 0.0, s, e * s)


def kernel(
    feat_ref, taps_ref, bias_ref, labels_ref,
    prob_ref, aff_ref,
    feat, lhs, lab, own, row19,
    y_low, y_high, z_low, z_high, low_low, low_high, high_low, high_high, row19_in,
    raw, edge, seed, w0, w1, w2,
    part, sum_z, sum_y,
    feat_sem, send_sem, recv_sem, psend_sem, precv_sem,
):
    gz, yx = lax.axis_index("gz"), lax.axis_index("yx")
    nz, ny = lax.axis_size("gz"), lax.axis_size("yx")
    z_up, z_dn = lax.rem(gz + 1, nz), lax.rem(gz + nz - 1, nz)
    y_up, y_dn = lax.rem(yx + 1, ny), lax.rem(yx + ny - 1, ny)

    loads = [
        pltpu.make_async_copy(feat_ref.at[c], feat.at[pl.ds(2, N), pl.ds(c * N, N), :], feat_sem.at[c])
        for c in range(CH)
    ]
    for load in loads:
        load.start()

    barrier = pltpu.get_barrier_semaphore()
    count = 0
    for dz in (z_dn, gz, z_up):
        for dy in (y_dn, yx, y_up):
            if dz is gz and dy is yx:
                continue
            pl.semaphore_signal(barrier, inc=1, device_id=(dz, dy), device_id_type=MESH)
            count += 1
    for i in range(2, nz - 1):
        pl.semaphore_signal(barrier, inc=1, device_id=(lax.rem(gz + i, nz), yx), device_id_type=MESH)
        count += 1
    for i in range(2, ny - 1):
        pl.semaphore_signal(barrier, inc=1, device_id=(gz, lax.rem(yx + i, ny)), device_id_type=MESH)
        count += 1

    for p in (0, 1, N + 2, N + 3):
        feat[p] = jnp.zeros((CH * N, X), jnp.bfloat16)
    lab[0] = jnp.zeros((N, X), F32)
    lab[N + 1] = jnp.zeros((N, X), F32)
    for z in range(N):
        lab[z + 1] = labels_ref[z].astype(F32)
    for z in range(N):
        row19[z : z + 1, :] = lab[z + 1, 3:4, :]
    build_weights(taps_ref, lhs)

    for load in loads:
        load.wait()

    sublane = row_iota((8, X))
    lane = lane_iota((8, X))
    first, last = lane == 0, lane == X - 1

    def two_planes(j, carry):
        plane = 2 * j
        left = feat[pl.ds(plane, 3)].reshape(3 * CH * N, X)
        right = feat[pl.ds(plane + 1, 3)].reshape(3 * CH * N, X)
        both = jnp.concatenate([left, right], axis=1)
        out = jnp.dot(lhs[...], both, preferred_element_type=F32)
        for h in range(2):
            for p in range((N + 2) // 2):
                at = 8 * p
                a = out[at : at + 8, h * X : (h + 1) * X]
                b = out[80 + at : 80 + at + 8, h * X : (h + 1) * X]
                c = out[160 + at : 160 + at + 8, h * X : (h + 1) * X]
                total = (
                    b
                    + jnp.where(first, 0.0, pltpu.roll(a, 1, 1))
                    + jnp.where(last, 0.0, pltpu.roll(c, X - 1, 1))
                )
                y = 2 * p - 1
                if y >= 0:
                    total = jnp.where(sublane == 3, spread_row(lab[plane + h, y : y + 1, :]), total)
                if y + 1 < N:
                    total = jnp.where(sublane == 7, spread_row(lab[plane + h, y + 1 : y + 2, :]), total)
                own[plane + h, at : at + 8, :] = total
        return carry

    lax.fori_loop(0, (N + 2) // 2, two_planes, 0)

    pl.semaphore_wait(barrier, count)

    bottom, top = pl.ds(0, 16), pl.ds(ROWS - 16, 16)
    sends = [
        (own.at[:, top, :], y_low, (gz, y_up)),
        (own.at[:, bottom, :], y_high, (gz, y_dn)),
        (own.at[pl.ds(N - 2, 4)], z_low, (z_up, yx)),
        (own.at[pl.ds(0, 5)], z_high, (z_dn, yx)),
        (own.at[pl.ds(N - 2, 4), top, :], low_low, (z_up, y_up)),
        (own.at[pl.ds(N - 2, 4), bottom, :], low_high, (z_up, y_dn)),
        (own.at[pl.ds(0, 4), top, :], high_low, (z_dn, y_up)),
        (own.at[pl.ds(0, 4), bottom, :], high_high, (z_dn, y_dn)),
        (row19, row19_in, (gz, y_dn)),
    ]
    copies = []
    for i, (src, dst, to) in enumerate(sends):
        copy = pltpu.make_async_remote_copy(
            src_ref=src, dst_ref=dst, send_sem=send_sem.at[i], recv_sem=recv_sem.at[i], device_id=to, device_id_type=MESH
        )
        copy.start()
        copies.append(copy)
    for copy in copies:
        copy.wait()

    has_zl, has_zh = (gz > 0).astype(F32), (gz < nz - 1).astype(F32)
    has_yl, has_yh = (yx > 0).astype(F32), (yx < ny - 1).astype(F32)
    kind = lax.rem(sublane, 4)
    bias = jnp.where(kind == 0, bias_ref[0], jnp.where(kind == 1, bias_ref[1], bias_ref[2]))
    keep_x = jnp.where((kind == 2) & last, 0.0, 1.0)
    is_label = kind == 3

    def plane_weights(plane, own_plane, zn, zn_plane, has_z, corner_low, corner_high, yn_plane):
        z = plane - LOW
        global_z = gz * N + z
        inside = jnp.logical_and(global_z >= 0, global_z < nz * N - 1).astype(F32)
        keep_zx = jnp.where(kind == 0, inside, keep_x)
        for v in range(11):
            terms = []
            if 1 <= v <= 9:
                if own_plane is not None:
                    terms.append(own[own_plane, 8 * (v - 1) : 8 * v, :])
                if zn is not None:
                    terms.append(has_z * zn[zn_plane, 8 * (v - 1) : 8 * v, :])
            if v <= 1:
                if yn_plane is not None:
                    terms.append(has_yl * y_low[yn_plane, 8 * v : 8 * v + 8, :])
                if corner_low is not None:
                    terms.append((has_yl * has_z) * corner_low[zn_plane, 8 * v : 8 * v + 8, :])
            if v >= 9:
                if yn_plane is not None:
                    terms.append(has_yh * y_high[yn_plane, 8 * (v - 9) : 8 * (v - 9) + 8, :])
                if corner_high is not None:
                    terms.append((has_yh * has_z) * corner_high[zn_plane, 8 * (v - 9) : 8 * (v - 9) + 8, :])
            total = terms[0]
            for term in terms[1:]:
                total = total + term
            a = jnp.where(is_label, total, sigmoid(total + bias))
            raw[plane, 8 * v : 8 * v + 8, :] = a
            keep = keep_zx
            if v == 1:
                keep = jnp.where(sublane == 1, has_yl, keep)
            if v == 9:
                keep = jnp.where(sublane == 1, has_yh, keep)
            edge[plane, 8 * v : 8 * v + 8, :] = jnp.where(is_label, (a == 0.0).astype(F32), a * keep)

    for z in (-3, -2):
        plane_weights(z + LOW, None, z_low, z + 3, has_zl, low_low, low_high, None)
    for z in (-1, 0):
        plane_weights(z + LOW, z + 1, z_low, z + 3, has_zl, low_low, low_high, z + 1)

    def middle(z, carry):
        plane_weights(z + LOW, z + 1, None, None, None, None, None, z + 1)
        return carry

    lax.fori_loop(1, N - 1, middle, 0)
    for z in (15, 16):
        plane_weights(z + LOW, z + 1, z_high, z - 15, has_zh, high_low, high_high, z + 1)
    for z in (17, 18):
        plane_weights(z + LOW, None, z_high, z - 15, has_zh, high_low, high_high, None)

    def affinities_out(z, carry):
        for o in range(3):
            for h in range(2):
                at = pl.multiple_of(o * N * N + z * N + 8 * h, 8)
                aff_ref[pl.ds(at, 8), :] = raw[z + LOW, pl.ds(4 * LOW + 32 * h + o, 8, stride=4), :]
        return carry

    lax.fori_loop(0, N, affinities_out, 0)

    colour = (sublane + 1).astype(F32)

    def seeds(plane, carry):
        for y in range(EXT - 1):
            label = spread_row(raw[plane, 4 * y + 3 : 4 * y + 4, :])
            seed[plane, y] = (label == colour).astype(F32)
        return carry

    lax.fori_loop(0, EXT - 1, seeds, 0)
    for z in range(N):
        seed[z + LOW, EXT - 1] = (spread_row(row19_in[z : z + 1, :]) == colour).astype(F32)
    for y in range(N):
        seed[EXT - 1, y + LOW] = (spread_row(z_high[4, 4 * y + 7 : 4 * y + 8, :]) == colour).astype(F32)

    zero = jnp.zeros((8, X), F32)

    def apply(src, dst, low, high, products):
        rows = range(low + LOW, high + LOW + 1)

        def weight(plane, y, o):
            return spread_row(edge[plane, 4 * y + o : 4 * y + o + 1, :])

        start = low + LOW
        below = [weight(start - 1, y, 0) * (src[start - 1, y] - src[start, y]) for y in rows]

        def step(plane, carry):
            below, sums = carry
            above = []
            y0 = rows[0]
            here = src[plane, y0]
            flux_y_before = weight(plane, y0 - 1, 1) * (src[plane, y0 - 1] - here)
            plane_sums = [zero] * len(products)
            for y in rows:
                after = src[plane, y + 1]
                flux_z = weight(plane, y, 0) * (here - src[plane + 1, y])
                flux_y = weight(plane, y, 1) * (here - after)
                flux_x = weight(plane, y, 2) * (here - pltpu.roll(here, X - 1, 1))
                total = (flux_z - below[y - y0]) + (flux_y - flux_y_before) + (flux_x - pltpu.roll(flux_x, 1, 1))
                result = weight(plane, y, 3) * total
                dst[plane, y] = result
                if LOW <= y < LOW + N:
                    for i, f in enumerate(products):
                        plane_sums[i] = plane_sums[i] + f(here, result)
                above.append(flux_z)
                here = after
                flux_y_before = flux_y
            mine = jnp.logical_and(plane >= LOW, plane < LOW + N).astype(F32)
            sums = tuple(s + mine * t for s, t in zip(sums, plane_sums))
            return tuple(above), sums

        _, sums = lax.fori_loop(start, high + LOW + 1, step, (tuple(below), (zero,) * len(products)))
        return sums

    def square(here, result):
        return result * result

    def cross(here, result):
        return here * result

    (m0,) = apply(seed, w0, -2, 18, [square])
    m1, m2 = apply(w0, w1, -1, 17, [cross, square])
    m3, m4 = apply(w1, w2, 0, 16, [cross, square])

    def energy(plane, total):
        here = w2[plane, LOW]
        for y in range(LOW, LOW + N):
            after = w2[plane, y + 1]
            d_z = here - w2[plane + 1, y]
            d_y = here - after
            d_x = here - pltpu.roll(here, X - 1, 1)
            total = total + (
                spread_row(edge[plane, 4 * y : 4 * y + 1, :]) * (d_z * d_z)
                + spread_row(edge[plane, 4 * y + 1 : 4 * y + 2, :]) * (d_y * d_y)
                + spread_row(edge[plane, 4 * y + 2 : 4 * y + 3, :]) * (d_x * d_x)
            )
            here = after
        return total

    m5 = lax.fori_loop(LOW, LOW + N, energy, zero)

    packed = zero
    for j, m in enumerate((m0, m1, m2, m3, m4, m5)):
        packed = jnp.where(lane == 8 * j + sublane, jnp.sum(m, axis=1, keepdims=True), packed)
    row = jnp.sum(packed, axis=0, keepdims=True)

    def all_sum(row, slots, me, count, stage, device):
        part[stage] = row
        slots[pl.ds(me, 1)] = row[None]
        copies = []
        for i in range(1, count):
            copy = pltpu.make_async_remote_copy(
                src_ref=part.at[stage], dst_ref=slots.at[me], send_sem=psend_sem.at[stage, i - 1],
                recv_sem=precv_sem.at[stage, i - 1], device_id=device(lax.rem(me + i, count)), device_id_type=MESH,
            )
            copy.start()
            copies.append(copy)
        for copy in copies:
            copy.wait()
        return jnp.sum(slots[...], axis=0)

    row = all_sum(row, sum_z, gz, nz, 0, lambda i: (i, yx))
    row = all_sum(row, sum_y, yx, ny, 1, lambda i: (gz, i))

    row = spread_row(row)
    mu = [
        jnp.broadcast_to(jnp.sum(jnp.where(lane == 8 * j + sublane, row, 0.0), axis=1, keepdims=True), (8, X))
        for j in range(6)
    ]

    def form(a, b, shift):
        total = None
        for i, p in enumerate(a):
            for j, q in enumerate(b):
                m = mu[i + j] if shift is None else mu[i + j + 1] + shift * mu[i + j]
                total = p * q * m if total is None else total + p * q * m
        return total

    one = jnp.ones((8, X), F32)
    residual, direction, answer = [one], [one], [zero] * ITERS
    rr = mu[0]
    for iteration in range(ITERS):
        length = jnp.clip(rr / form(direction, direction, RIDGE), STEP_LOW, STEP_HIGH)
        for i, d in enumerate(direction):
            answer[i] = answer[i] + length * d
        if iteration + 1 == ITERS:
            break
        shifted = [zero] + direction
        applied = [RIDGE * d + s for d, s in zip(direction + [zero], shifted)]
        residual = [r - length * a for r, a in zip(residual + [zero], applied)]
        after = form(residual, residual, None)
        beta = jnp.clip(after / rr, 0.0, BETA_HIGH)
        direction = [r + beta * d for r, d in zip(residual, direction + [zero])]
        rr = after

    def finish(z, carry):
        for y in range(N):
            at = (z + LOW, y + LOW)
            value = seed[at] - (answer[0] * w0[at] + answer[1] * w1[at] + answer[2] * w2[at])
            prob_ref[pl.ds(z * N + y, FIELDS, stride=N * N), :] = value
        return carry

    lax.fori_loop(0, N, finish, 0)


def body(features, conv_weight, conv_bias, labels):
    taps = jnp.pad(conv_weight.transpose(3, 4, 0, 2, 1), ((0, 0), (0, 0), (0, 1), (0, 0), (0, 0)))
    taps = jnp.concatenate([taps, taps], axis=2).reshape(72, 3 * CH)
    vmem = pl.BlockSpec(memory_space=pltpu.VMEM)
    strips = [
        pltpu.VMEM((N + 2, 16, X), F32), pltpu.VMEM((N + 2, 16, X), F32),
        pltpu.VMEM((4, ROWS, X), F32), pltpu.VMEM((5, ROWS, X), F32),
        pltpu.VMEM((4, 16, X), F32), pltpu.VMEM((4, 16, X), F32),
        pltpu.VMEM((4, 16, X), F32), pltpu.VMEM((4, 16, X), F32),
        pltpu.VMEM((N, X), F32),
    ]
    prob, aff = pl.pallas_call(
        kernel,
        out_shape=(
            jax.ShapeDtypeStruct((FIELDS * N * N, X), F32),
            jax.ShapeDtypeStruct((3 * N * N, X), F32),
        ),
        in_specs=[pl.BlockSpec(memory_space=pl.ANY), vmem, pl.BlockSpec(memory_space=pltpu.SMEM), vmem],
        out_specs=(vmem, vmem),
        scratch_shapes=[
            pltpu.VMEM((N + 4, CH * N, X), jnp.bfloat16),
            pltpu.VMEM((240, 3 * CH * N), jnp.bfloat16),
            pltpu.VMEM((N + 2, N, X), F32),
            pltpu.VMEM((N + 2, ROWS, X), F32),
            pltpu.VMEM((N, X), F32),
            *strips,
            pltpu.VMEM((EXT, 96, X), F32),
            pltpu.VMEM((EXT, 96, X), F32),
            pltpu.VMEM((EXT, EXT, 8, X), F32),
            pltpu.VMEM((EXT, EXT, 8, X), F32),
            pltpu.VMEM((EXT, EXT, 8, X), F32),
            pltpu.VMEM((EXT, EXT, 8, X), F32),
            pltpu.VMEM((2, 1, X), F32),
            pltpu.VMEM((8, 1, X), F32),
            pltpu.VMEM((32, 1, X), F32),
            pltpu.SemaphoreType.DMA((CH,)),
            pltpu.SemaphoreType.DMA((9,)),
            pltpu.SemaphoreType.DMA((9,)),
            pltpu.SemaphoreType.DMA((2, 31)),
            pltpu.SemaphoreType.DMA((2, 31)),
        ],
        compiler_params=pltpu.CompilerParams(collective_id=0, has_side_effects=True, vmem_limit_bytes=40 * 2**20),
    )(features, taps, conv_bias, labels)
    return prob.reshape(FIELDS, N, N, X), aff.reshape(3, N, N, X)


def solution(mesh):
    in_specs = (P(None, "gz", "yx", None), P(), P(), P("gz", "yx", None))
    out_specs = (P(None, "gz", "yx", None), P(None, "gz", "yx", None))
    return jax.shard_map(body, mesh=mesh, in_specs=in_specs, out_specs=out_specs, check_vma=False)
```

```python
import jax
import jax.numpy as jnp
from jax import lax
from jax.experimental import pallas as pl
from jax.experimental.pallas import tpu as pltpu
from jax.sharding import PartitionSpec as P

FEATURE_ORDER = (*range(6), *range(10, 16), *range(6, 10))
MESH = pl.DeviceIdType.MESH
FIELDS = 8
ITERS = 3
RIDGE = 0.5
N = 16
X = 128
CH = 16
LOW = 3
EXT = N + 7
ROWS = 4 * (N + 2)
F32 = jnp.float32

STEP_LOW, STEP_HIGH = 1.0 / 12.5, 2.0
BETA_HIGH = 25.0


def lane_iota(shape):
    return lax.broadcasted_iota(jnp.int32, shape, len(shape) - 1)


def row_iota(shape):
    return lax.broadcasted_iota(jnp.int32, shape, len(shape) - 2)


def spread_row(row):
    return jnp.broadcast_to(row, (8, X))


def build_weights(conv_ref, rows_ref, taps_ref, lhs_ref):
    rows_ref[...] = jnp.zeros_like(rows_ref)
    for o in range(3):
        for dz in range(3):
            for dy in range(3):
                at = ((o * 3 + dz) * 3 + dy) * 3
                rows_ref[at : at + 3, 0:CH] = conv_ref[o, dz, dy].astype(F32)
    expand = (lax.div(lane_iota((X, CH * N)), N) == row_iota((X, CH * N))).astype(jnp.bfloat16)
    taps_ref[...] = jnp.dot(rows_ref[...].astype(jnp.bfloat16), expand, preferred_element_type=F32)
    columns = CH * N
    y_in = lax.rem(lane_iota((8, columns)), N)
    kind = lax.rem(row_iota((8, columns)), 4)
    half = lax.div(row_iota((8, columns)), 4)
    for dx in range(3):
        for dz in range(3):
            taps = []
            for dy in range(3):
                tap = jnp.zeros((8, columns), F32)
                for o in range(3):
                    at = ((o * 3 + dz) * 3 + dy) * 3 + dx
                    tap = jnp.where(kind == o, jnp.broadcast_to(taps_ref[at : at + 1, :], (8, columns)), tap)
                taps.append(tap)
            for pair in range(0, (N + 2) // 2, 2):
                blocks = []
                for p in (pair, pair + 1):
                    block = jnp.zeros((8, columns), F32)
                    if p < (N + 2) // 2:
                        gap = y_in - (2 * p - 1 + half) + 1
                        for dy in range(3):
                            block = jnp.where(gap == dy, taps[dy], block)
                    blocks.append(block)
                at = dx * 80 + pair * 8
                lhs_ref[at : at + 16, dz * columns : (dz + 1) * columns] = jnp.concatenate(blocks, axis=0).astype(jnp.bfloat16)


def sigmoid(x):
    e = jnp.exp(-jnp.abs(x))
    s = 1.0 / (1.0 + e)
    return jnp.where(x >= 0.0, s, e * s)


def kernel(
    feat_ref, conv_ref, bias_ref, labels_ref,
    basis_ref, answer_ref, aff_ref,
    conv, bias_v, feat, taps_rows, taps, lhs, labels, lab, own, row19,
    y_low, y_high, z_low, z_high, low_low, low_high, high_low, high_high, row19_in,
    raw, edge, mark, mark_left, mark_right, w0, w1, w2,
    part, sum_z, sum_y, aff_v, answer_v,
    feat_sem, label_sem, small_sem, out_sem, send_sem, recv_sem, psend_sem, precv_sem,
):
    gz, yx = lax.axis_index("gz"), lax.axis_index("yx")
    nz, ny = lax.axis_size("gz"), lax.axis_size("yx")
    z_up, z_dn = lax.rem(gz + 1, nz), lax.rem(gz + nz - 1, nz)
    y_up, y_dn = lax.rem(yx + 1, ny), lax.rem(yx + ny - 1, ny)

    barrier = pltpu.get_barrier_semaphore()
    count = 0
    for dz in (z_dn, gz, z_up):
        for dy in (y_dn, yx, y_up):
            if dz is gz and dy is yx:
                continue
            pl.semaphore_signal(barrier, inc=1, device_id=(dz, dy), device_id_type=MESH)
            count += 1
    for i in range(2, nz - 1):
        pl.semaphore_signal(barrier, inc=1, device_id=(lax.rem(gz + i, nz), yx), device_id_type=MESH)
        count += 1
    for i in range(2, ny - 1):
        pl.semaphore_signal(barrier, inc=1, device_id=(gz, lax.rem(yx + i, ny)), device_id_type=MESH)
        count += 1

    load_conv = pltpu.make_async_copy(conv_ref, conv, small_sem.at[0])
    load_bias = pltpu.make_async_copy(bias_ref, bias_v, small_sem.at[1])
    load_conv.start()
    load_bias.start()
    loads = [
        pltpu.make_async_copy(feat_ref.at[:, z], feat.at[z + 2], feat_sem.at[z])
        for z in range(N)
    ]
    load_labels = pltpu.make_async_copy(labels_ref, labels, label_sem)
    load_labels.start()
    for z in FEATURE_ORDER:
        loads[z].start()

    for p in (0, 1, N + 2, N + 3):
        feat[p] = jnp.zeros((CH, N, X), jnp.bfloat16)
    lab[0] = jnp.zeros((N, X), F32)
    lab[N + 1] = jnp.zeros((N, X), F32)
    load_conv.wait()
    load_bias.wait()
    build_weights(conv, taps_rows, taps, lhs)
    load_labels.wait()
    for z in range(N):
        lab[z + 1] = labels[z].astype(F32)
    for z in range(N):
        row19[z : z + 1, :] = lab[z + 1, 3:4, :]

    sublane = row_iota((8, X))
    lane = lane_iota((8, X))
    first, last = lane == 0, lane == X - 1
    zero = jnp.zeros((8, X), F32)

    def two_planes(j):
        plane = 2 * j
        left = feat[pl.ds(plane, 3)].reshape(3 * CH * N, X)
        right = feat[pl.ds(plane + 1, 3)].reshape(3 * CH * N, X)
        both = jnp.concatenate([left, right], axis=1)
        out = jnp.dot(lhs[...], both, preferred_element_type=F32)
        for h in range(2):
            for p in range((N + 2) // 2):
                at = 8 * p
                a = out[at : at + 8, h * X : (h + 1) * X]
                b = out[80 + at : 80 + at + 8, h * X : (h + 1) * X]
                c = out[160 + at : 160 + at + 8, h * X : (h + 1) * X]
                total = (
                    b
                    + jnp.where(first, 0.0, pltpu.roll(a, 1, 1))
                    + jnp.where(last, 0.0, pltpu.roll(c, X - 1, 1))
                )
                y = 2 * p - 1
                if y >= 0:
                    total = jnp.where(sublane == 3, spread_row(lab[plane + h, y : y + 1, :]), total)
                if y + 1 < N:
                    total = jnp.where(sublane == 7, spread_row(lab[plane + h, y + 1 : y + 2, :]), total)
                own[plane + h, at : at + 8, :] = total

    copies = []

    def send(src, dst, to):
        i = len(copies)
        copy = pltpu.make_async_remote_copy(
            src_ref=src, dst_ref=dst, send_sem=send_sem.at[i], recv_sem=recv_sem.at[i], device_id=to, device_id_type=MESH
        )
        copy.start()
        copies.append(copy)

    bottom, top = pl.ds(0, 16), pl.ds(ROWS - 16, 16)
    here = set()
    for chunk, pairs in enumerate(((0, 1, 2), (6, 7, 8), (3, 4, 5))):
        for z in FEATURE_ORDER:
            if z not in here and 2 * pairs[0] - 2 <= z <= 2 * pairs[-1] + 1:
                loads[z].wait()
                here.add(z)
        for j in pairs:
            two_planes(j)
        if chunk == 0:
            pl.semaphore_wait(barrier, count)
            send(row19, row19_in, (gz, y_dn))
        six = pl.ds(2 * pairs[0], 6)
        send(own.at[six, top, :], y_low.at[six], (gz, y_up))
        send(own.at[six, bottom, :], y_high.at[six], (gz, y_dn))
        if chunk == 0:
            send(own.at[pl.ds(0, 5)], z_high, (z_dn, yx))
            send(own.at[pl.ds(0, 4), top, :], high_low, (z_dn, y_up))
            send(own.at[pl.ds(0, 4), bottom, :], high_high, (z_dn, y_dn))
        if chunk == 1:
            send(own.at[pl.ds(N - 2, 4)], z_low, (z_up, yx))
            send(own.at[pl.ds(N - 2, 4), top, :], low_low, (z_up, y_up))
            send(own.at[pl.ds(N - 2, 4), bottom, :], low_high, (z_up, y_dn))

    has_zl, has_zh = (gz > 0).astype(F32), (gz < nz - 1).astype(F32)
    has_yl, has_yh = (yx > 0).astype(F32), (yx < ny - 1).astype(F32)
    kind = lax.rem(sublane, 4)
    bias = zero
    for o in range(3):
        bias = jnp.where(kind == o, jnp.broadcast_to(bias_v[0:1, o : o + 1], (8, X)), bias)
    keep_x = jnp.where((kind == 2) & last, 0.0, 1.0)
    is_label = kind == 3

    def plane_weights(plane, own_plane, zn, zn_plane, has_z, corner_low, corner_high, yn_plane, rows=range(11)):
        z = plane - LOW
        global_z = gz * N + z
        inside = jnp.logical_and(global_z >= 0, global_z < nz * N - 1).astype(F32)
        keep_zx = jnp.where(kind == 0, inside, keep_x)
        for v in rows:
            terms = []
            if 1 <= v <= 9:
                if own_plane is not None:
                    terms.append(own[own_plane, 8 * (v - 1) : 8 * v, :])
                if zn is not None:
                    terms.append(has_z * zn[zn_plane, 8 * (v - 1) : 8 * v, :])
            if v <= 1:
                if yn_plane is not None:
                    terms.append(has_yl * y_low[yn_plane, 8 * v : 8 * v + 8, :])
                if corner_low is not None:
                    terms.append((has_yl * has_z) * corner_low[zn_plane, 8 * v : 8 * v + 8, :])
            if v >= 9:
                if yn_plane is not None:
                    terms.append(has_yh * y_high[yn_plane, 8 * (v - 9) : 8 * (v - 9) + 8, :])
                if corner_high is not None:
                    terms.append((has_yh * has_z) * corner_high[zn_plane, 8 * (v - 9) : 8 * (v - 9) + 8, :])
            total = terms[0]
            for term in terms[1:]:
                total = total + term
            a = sigmoid(total + bias)
            raw[plane, 8 * v : 8 * v + 8, :] = jnp.where(is_label, (total == 0.0).astype(F32), a)
            mark[plane, 8 * v : 8 * v + 8, :] = total
            mark_right[plane, 8 * v : 8 * v + 8, :] = pltpu.roll(total, X - 1, 1)
            keep = keep_zx
            if v == 1:
                keep = jnp.where(sublane == 1, has_yl, keep)
            if v == 9:
                keep = jnp.where(sublane == 1, has_yh, keep)
            kept = a * keep
            before = pltpu.roll(jnp.where(is_label, total, kept), 1, 1)
            mark_left[plane, 8 * v : 8 * v + 8, :] = before
            edge[plane, 8 * v : 8 * v + 8, :] = jnp.where(is_label, pltpu.roll(before, 1, 0), kept)

    def middle(rows, carry):
        def step(z, carry):
            plane_weights(z + LOW, z + 1, None, None, None, None, None, z + 1, rows)
            return carry

        lax.fori_loop(1, N - 1, step, carry)

    middle(range(2, 9), 0)
    for copy in copies:
        copy.wait()
    middle((0, 1, 9, 10), 0)
    for z in (-3, -2):
        plane_weights(z + LOW, None, z_low, z + 3, has_zl, low_low, low_high, None)
    for z in (-1, 0):
        plane_weights(z + LOW, z + 1, z_low, z + 3, has_zl, low_low, low_high, z + 1)
    for z in (15, 16):
        plane_weights(z + LOW, z + 1, z_high, z - 15, has_zh, high_low, high_high, z + 1)
    for z in (17, 18):
        plane_weights(z + LOW, None, z_high, z - 15, has_zh, high_low, high_high, None)

    def affinities_out(z, carry):
        for o in range(3):
            for h in range(2):
                at = pl.multiple_of(o * N * N + z * N + 8 * h, 8)
                aff_v[pl.ds(at, 8), :] = raw[z + LOW, pl.ds(4 * LOW + 32 * h + o, 8, stride=4), :]
        return carry

    lax.fori_loop(0, N, affinities_out, 0)
    stores = [pltpu.make_async_copy(aff_v, aff_ref, out_sem.at[0])]
    stores[-1].start()

    for z in range(N):
        mark[z + LOW, 4 * (EXT - 1) + 3 : 4 * EXT, :] = row19_in[z : z + 1, :]
    mark[EXT - 1, 8 : 8 + ROWS, :] = z_high[4]

    colour = (sublane + 1).astype(F32)

    def weight(plane, y, o):
        return spread_row(edge[plane, 4 * y + o : 4 * y + o + 1, :])

    def unseeded(plane, y):
        return spread_row(raw[plane, 4 * y + 3 : 4 * y + 4, :])

    def planes(body, low, high, group, carry):
        start, count = low + LOW, high - low + 1

        def step(i, carry):
            for g in range(group):
                carry = body(start + i * group + g, carry)
            return carry

        carry = lax.fori_loop(0, count // group, step, carry)
        for plane in range(start + count // group * group, start + count):
            carry = body(plane, carry)
        return carry

    def in_block(plane):
        return jnp.logical_and(plane >= LOW, plane < LOW + N).astype(F32)

    def first_step(plane, m0):
        plane_sum = zero
        before_w = weight(plane, 0, 1)
        for y in range(LOW - 2, LOW + N + 3):
            at = 4 * y + 3
            after_w = weight(plane, y, 1)
            total = zero
            for marks, where, w in (
                (mark, (plane - 1, at), weight(plane - 1, y, 0)),
                (mark, (plane + 1, at), weight(plane, y, 0)),
                (mark, (plane, at - 4), before_w),
                (mark, (plane, at + 4), after_w),
                (mark_left, (plane, at), weight(plane, y, 3)),
                (mark_right, (plane, at), weight(plane, y, 2)),
            ):
                label = spread_row(marks[where[0], where[1] : where[1] + 1, :])
                total = total - jnp.where(label == colour, w, 0.0)
            result = unseeded(plane, y) * total
            w0[plane, y] = result
            if LOW <= y < LOW + N:
                plane_sum = plane_sum + result * result
            before_w = after_w
        return m0 + in_block(plane) * plane_sum

    def store_block(i, w):
        inner = pl.ds(LOW, N)
        copy = pltpu.make_async_copy(w.at[inner, inner], basis_ref.at[i], out_sem.at[i + 1])
        copy.start()
        stores.append(copy)

    m0 = planes(first_step, -2, 18, 3, zero)
    store_block(0, w0)

    def apply(src, dst, low, high, group):
        rows = range(low + LOW, high + LOW + 1)
        y0 = rows[0]

        def step(plane, carry):
            below, crosses, squares = carry
            above = []
            here = src[plane, y0]
            flux_y_before = weight(plane, y0 - 1, 1) * (src[plane, y0 - 1] - here)
            cross = square = zero
            for y in rows:
                after = src[plane, y + 1]
                flux_z = weight(plane, y, 0) * (here - src[plane + 1, y])
                flux_y = weight(plane, y, 1) * (here - after)
                right = weight(plane, y, 2) * (here - pltpu.roll(here, X - 1, 1))
                left = weight(plane, y, 3) * (here - pltpu.roll(here, 1, 1))
                total = ((flux_z - below[y - y0]) + (flux_y - flux_y_before)) + (right + left)
                result = unseeded(plane, y) * total
                dst[plane, y] = result
                if LOW <= y < LOW + N:
                    cross = cross + here * result
                    square = square + result * result
                above.append(flux_z)
                here = after
                flux_y_before = flux_y
            mine = in_block(plane)
            return tuple(above), crosses + mine * cross, squares + mine * square

        start = low + LOW
        below = tuple(weight(start - 1, y, 0) * (src[start - 1, y] - src[start, y]) for y in rows)
        return planes(step, low, high, group, (below, zero, zero))[1:]

    m1, m2 = apply(w0, w1, -1, 17, 3)
    store_block(1, w1)
    m3, m4 = apply(w1, w2, 0, 16, 3)
    store_block(2, w2)

    def energy(plane, total):
        here = w2[plane, LOW]
        sums = zero
        for y in range(LOW, LOW + N):
            after = w2[plane, y + 1]
            d_z = here - w2[plane + 1, y]
            d_y = here - after
            d_x = here - pltpu.roll(here, X - 1, 1)
            sums = sums + (
                weight(plane, y, 0) * (d_z * d_z) + weight(plane, y, 1) * (d_y * d_y) + weight(plane, y, 2) * (d_x * d_x)
            )
            here = after
        return total + sums

    m5 = planes(energy, 0, N - 1, 4, zero)

    packed = zero
    for j, m in enumerate((m0, m1, m2, m3, m4, m5)):
        packed = jnp.where(lane == 8 * j + sublane, jnp.sum(m, axis=1, keepdims=True), packed)
    row = jnp.sum(packed, axis=0, keepdims=True)

    def all_sum(row, slots, me, count, stage, device):
        part[stage] = row
        slots[pl.ds(me, 1)] = row[None]
        copies = []
        for i in range(1, count):
            copy = pltpu.make_async_remote_copy(
                src_ref=part.at[stage], dst_ref=slots.at[me], send_sem=psend_sem.at[stage, i - 1],
                recv_sem=precv_sem.at[stage, i - 1], device_id=device(lax.rem(me + i, count)), device_id_type=MESH,
            )
            copy.start()
            copies.append(copy)
        for copy in copies:
            copy.wait()
        return jnp.sum(slots[...], axis=0)

    row = all_sum(row, sum_z, gz, nz, 0, lambda i: (i, yx))
    row = all_sum(row, sum_y, yx, ny, 1, lambda i: (gz, i))

    row = spread_row(row)
    mu = [
        jnp.broadcast_to(jnp.sum(jnp.where(lane == 8 * j + sublane, row, 0.0), axis=1, keepdims=True), (8, X))
        for j in range(6)
    ]

    def form(a, b, shift):
        total = None
        for i, p in enumerate(a):
            for j, q in enumerate(b):
                m = mu[i + j] if shift is None else mu[i + j + 1] + shift * mu[i + j]
                total = p * q * m if total is None else total + p * q * m
        return total

    one = jnp.ones((8, X), F32)
    residual, direction, answer = [one], [one], [zero] * ITERS
    rr = mu[0]
    for iteration in range(ITERS):
        length = jnp.clip(rr / form(direction, direction, RIDGE), STEP_LOW, STEP_HIGH)
        for i, d in enumerate(direction):
            answer[i] = answer[i] + length * d
        if iteration + 1 == ITERS:
            break
        shifted = [zero] + direction
        applied = [RIDGE * d + s for d, s in zip(direction + [zero], shifted)]
        residual = [r - length * a for r, a in zip(residual + [zero], applied)]
        after = form(residual, residual, None)
        beta = jnp.clip(after / rr, 0.0, BETA_HIGH)
        direction = [r + beta * d for r, d in zip(residual, direction + [zero])]
        rr = after

    for i in range(ITERS):
        answer_v[i] = answer[i]
    copy = pltpu.make_async_copy(answer_v, answer_ref, out_sem.at[4])
    copy.start()
    stores.append(copy)
    for copy in stores:
        copy.wait()


CHUNKS = 2
DEEP = N // CHUNKS


def finish_kernel(basis_ref, answer_ref, labels_ref, aff_in_ref, prob_ref, aff_ref, basis, answer, labels, prob, aff_v, in_sem, small_sem, out_sem):
    affinities = pltpu.make_async_copy(aff_in_ref, aff_v, small_sem.at[2])
    small = [
        pltpu.make_async_copy(answer_ref, answer, small_sem.at[0]),
        pltpu.make_async_copy(labels_ref, labels, small_sem.at[1]),
    ]
    for copy in small:
        copy.start()
    loads = []
    for j in range(CHUNKS):
        part = pl.ds(j * DEEP, DEEP)
        load = pltpu.make_async_copy(basis_ref.at[:, part], basis.at[:, part], in_sem.at[j])
        load.start()
        loads.append(load)
    affinities.start()
    for copy in small:
        copy.wait()
    colour = row_iota((8, X)) + 1
    a, b, c = (answer[i] for i in range(ITERS))
    stores = []
    for j in range(CHUNKS):
        loads[j].wait()

        def plane(z, carry):
            for y in range(N):
                seed = jnp.where(spread_row(labels[z, y : y + 1, :]) == colour, 1.0, 0.0)
                value = seed - (a * basis[0, z, y] + b * basis[1, z, y] + c * basis[2, z, y])
                prob[pl.ds(z * N + y, FIELDS, stride=N * N), :] = value
            return carry

        lax.fori_loop(j * DEEP, (j + 1) * DEEP, plane, 0)
        part = pl.ds(j * DEEP * N, DEEP * N)
        copy = pltpu.make_async_copy(prob.reshape(FIELDS, N * N, X).at[:, part], prob_ref.at[:, part], out_sem.at[j])
        copy.start()
        stores.append(copy)
        if j == 0:
            affinities.wait()
            affinities = pltpu.make_async_copy(aff_v, aff_ref, small_sem.at[2])
            affinities.start()
    stores.append(affinities)
    for copy in stores:
        copy.wait()


def body(features, conv_weight, conv_bias, labels):
    taps = conv_weight.transpose(0, 2, 3, 4, 1)
    vmem = pl.BlockSpec(memory_space=pltpu.VMEM)
    hbm = pl.BlockSpec(memory_space=pltpu.HBM)
    strips = [
        pltpu.VMEM((N + 2, 16, X), F32), pltpu.VMEM((N + 2, 16, X), F32),
        pltpu.VMEM((4, ROWS, X), F32), pltpu.VMEM((5, ROWS, X), F32),
        pltpu.VMEM((4, 16, X), F32), pltpu.VMEM((4, 16, X), F32),
        pltpu.VMEM((4, 16, X), F32), pltpu.VMEM((4, 16, X), F32),
        pltpu.VMEM((N, X), F32),
    ]
    basis, answer, aff = pl.pallas_call(
        kernel,
        out_shape=(
            jax.ShapeDtypeStruct((ITERS, N, N, FIELDS, X), F32),
            jax.ShapeDtypeStruct((ITERS, FIELDS, X), F32),
            jax.ShapeDtypeStruct((3 * N * N, X), F32),
        ),
        in_specs=[hbm] * 4,
        out_specs=(hbm,) * 3,
        scratch_shapes=[
            pltpu.VMEM((3, 3, 3, 3, CH), jnp.bfloat16),
            pltpu.VMEM((1, 3), F32),
            pltpu.VMEM((N + 4, CH, N, X), jnp.bfloat16),
            pltpu.VMEM((96, X), F32),
            pltpu.VMEM((96, CH * N), F32),
            pltpu.VMEM((240, 3 * CH * N), jnp.bfloat16),
            pltpu.VMEM((N, N, X), jnp.int32),
            pltpu.VMEM((N + 2, N, X), F32),
            pltpu.VMEM((N + 2, ROWS, X), F32),
            pltpu.VMEM((N, X), F32),
            *strips,
            pltpu.VMEM((EXT, 96, X), F32),
            pltpu.VMEM((EXT, 96, X), F32),
            pltpu.VMEM((EXT, 96, X), F32),
            pltpu.VMEM((EXT, 96, X), F32),
            pltpu.VMEM((EXT, 96, X), F32),
            pltpu.VMEM((EXT, EXT, 8, X), F32),
            pltpu.VMEM((EXT, EXT, 8, X), F32),
            pltpu.VMEM((EXT, EXT, 8, X), F32),
            pltpu.VMEM((2, 1, X), F32),
            pltpu.VMEM((8, 1, X), F32),
            pltpu.VMEM((32, 1, X), F32),
            pltpu.VMEM((3 * N * N, X), F32),
            pltpu.VMEM((ITERS, FIELDS, X), F32),
            pltpu.SemaphoreType.DMA((N,)),
            pltpu.SemaphoreType.DMA,
            pltpu.SemaphoreType.DMA((2,)),
            pltpu.SemaphoreType.DMA((5,)),
            pltpu.SemaphoreType.DMA((13,)),
            pltpu.SemaphoreType.DMA((13,)),
            pltpu.SemaphoreType.DMA((2, 31)),
            pltpu.SemaphoreType.DMA((2, 31)),
        ],
        compiler_params=pltpu.CompilerParams(collective_id=0, has_side_effects=True, vmem_limit_bytes=60 * 2**20),
    )(features, taps, conv_bias[None], labels)
    prob, aff = pl.pallas_call(
        finish_kernel,
        out_shape=(jax.ShapeDtypeStruct((FIELDS, N * N, X), F32), jax.ShapeDtypeStruct((3 * N * N, X), F32)),
        in_specs=[hbm] * 4,
        out_specs=(hbm, hbm),
        scratch_shapes=[
            pltpu.VMEM((ITERS, N, N, FIELDS, X), F32),
            pltpu.VMEM((ITERS, FIELDS, X), F32),
            pltpu.VMEM((N, N, X), jnp.int32),
            pltpu.VMEM((FIELDS * N * N, X), F32),
            pltpu.VMEM((3 * N * N, X), F32),
            pltpu.SemaphoreType.DMA((CHUNKS,)),
            pltpu.SemaphoreType.DMA((3,)),
            pltpu.SemaphoreType.DMA((CHUNKS,)),
        ],
        compiler_params=pltpu.CompilerParams(vmem_limit_bytes=60 * 2**20),
    )(basis, answer, labels, aff)
    return prob.reshape(FIELDS, N, N, X), aff.reshape(3, N, N, X)


def solution(mesh):
    in_specs = (P(None, "gz", "yx", None), P(), P(), P("gz", "yx", None))
    out_specs = (P(None, "gz", "yx", None), P(None, "gz", "yx", None))
    return jax.shard_map(body, mesh=mesh, in_specs=in_specs, out_specs=out_specs, check_vma=False)
```

```python
import jax
import jax.numpy as jnp
from jax import lax
from jax.experimental import pallas as pl
from jax.experimental.pallas import tpu as pltpu
from jax.sharding import PartitionSpec as P

FEATURE_ORDER = (*range(6), *range(10, 16), *range(6, 10))
MESH = pl.DeviceIdType.MESH
FIELDS = 8
ITERS = 3
RIDGE = 0.5
N = 16
X = 128
CH = 16
LOW = 3
EXT = N + 7
ROWS = 4 * (N + 2)
F32 = jnp.float32

STEP_LOW, STEP_HIGH = 1.0 / 12.5, 2.0
BETA_HIGH = 25.0


def lane_iota(shape):
    return lax.broadcasted_iota(jnp.int32, shape, len(shape) - 1)


def row_iota(shape):
    return lax.broadcasted_iota(jnp.int32, shape, len(shape) - 2)


def spread_row(row):
    return jnp.broadcast_to(row, (8, X))


def build_weights(conv_ref, rows_ref, taps_ref, lhs_ref):
    rows_ref[...] = jnp.zeros_like(rows_ref)
    for o in range(3):
        for dz in range(3):
            for dy in range(3):
                at = ((o * 3 + dz) * 3 + dy) * 3
                rows_ref[at : at + 3, 0:CH] = conv_ref[o, dz, dy].astype(F32)
    expand = (lax.div(lane_iota((X, CH * N)), N) == row_iota((X, CH * N))).astype(jnp.bfloat16)
    taps_ref[...] = jnp.dot(rows_ref[...].astype(jnp.bfloat16), expand, preferred_element_type=F32)
    columns = CH * N
    y_in = lax.rem(lane_iota((8, columns)), N)
    kind = lax.rem(row_iota((8, columns)), 4)
    half = lax.div(row_iota((8, columns)), 4)
    for dx in range(3):
        for dz in range(3):
            taps = []
            for dy in range(3):
                tap = jnp.zeros((8, columns), F32)
                for o in range(3):
                    at = ((o * 3 + dz) * 3 + dy) * 3 + dx
                    tap = jnp.where(kind == o, jnp.broadcast_to(taps_ref[at : at + 1, :], (8, columns)), tap)
                taps.append(tap)
            for pair in range(0, (N + 2) // 2, 2):
                blocks = []
                for p in (pair, pair + 1):
                    block = jnp.zeros((8, columns), F32)
                    if p < (N + 2) // 2:
                        gap = y_in - (2 * p - 1 + half) + 1
                        for dy in range(3):
                            block = jnp.where(gap == dy, taps[dy], block)
                    blocks.append(block)
                at = dx * 80 + pair * 8
                lhs_ref[at : at + 16, dz * columns : (dz + 1) * columns] = jnp.concatenate(blocks, axis=0).astype(jnp.bfloat16)


def sigmoid(x):
    e = jnp.exp(-jnp.abs(x))
    s = 1.0 / (1.0 + e)
    return jnp.where(x >= 0.0, s, e * s)


def kernel(
    feat_ref, conv_ref, bias_ref, labels_ref,
    basis_ref, answer_ref, aff_ref,
    conv, bias_v, feat, taps_rows, taps, lhs, labels, lab, own, row19,
    y_low, y_high, z_low, z_high, low_low, low_high, high_low, high_high, row19_in,
    raw, edge, mark, mark_left, mark_right, w0, w1, w2,
    part, sum_z, sum_y, aff_v, answer_v,
    feat_sem, label_sem, small_sem, out_sem, send_sem, recv_sem, psend_sem, precv_sem,
):
    gz, yx = lax.axis_index("gz"), lax.axis_index("yx")
    nz, ny = lax.axis_size("gz"), lax.axis_size("yx")
    z_up, z_dn = lax.rem(gz + 1, nz), lax.rem(gz + nz - 1, nz)
    y_up, y_dn = lax.rem(yx + 1, ny), lax.rem(yx + ny - 1, ny)

    barrier = pltpu.get_barrier_semaphore()
    count = 0
    for dz in (z_dn, gz, z_up):
        for dy in (y_dn, yx, y_up):
            if dz is gz and dy is yx:
                continue
            pl.semaphore_signal(barrier, inc=1, device_id=(dz, dy), device_id_type=MESH)
            count += 1
    for i in range(2, nz - 1):
        pl.semaphore_signal(barrier, inc=1, device_id=(lax.rem(gz + i, nz), yx), device_id_type=MESH)
        count += 1
    for i in range(2, ny - 1):
        pl.semaphore_signal(barrier, inc=1, device_id=(gz, lax.rem(yx + i, ny)), device_id_type=MESH)
        count += 1

    load_conv = pltpu.make_async_copy(conv_ref, conv, small_sem.at[0])
    load_bias = pltpu.make_async_copy(bias_ref, bias_v, small_sem.at[1])
    load_conv.start()
    load_bias.start()
    loads = [
        pltpu.make_async_copy(feat_ref.at[:, z], feat.at[z + 2], feat_sem.at[z])
        for z in range(N)
    ]
    load_labels = pltpu.make_async_copy(labels_ref, labels, label_sem)
    load_labels.start()
    for z in FEATURE_ORDER:
        loads[z].start()

    for p in (0, 1, N + 2, N + 3):
        feat[p] = jnp.zeros((CH, N, X), jnp.bfloat16)
    lab[0] = jnp.zeros((N, X), F32)
    lab[N + 1] = jnp.zeros((N, X), F32)
    load_conv.wait()
    load_bias.wait()
    build_weights(conv, taps_rows, taps, lhs)
    load_labels.wait()
    for z in range(N):
        lab[z + 1] = labels[z].astype(F32)
    for z in range(N):
        row19[z : z + 1, :] = lab[z + 1, 3:4, :]

    sublane = row_iota((8, X))
    lane = lane_iota((8, X))
    first, last = lane == 0, lane == X - 1
    zero = jnp.zeros((8, X), F32)

    def two_planes(j):
        plane = 2 * j
        left = feat[pl.ds(plane, 3)].reshape(3 * CH * N, X)
        right = feat[pl.ds(plane + 1, 3)].reshape(3 * CH * N, X)
        both = jnp.concatenate([left, right], axis=1)
        out = jnp.dot(lhs[...], both, preferred_element_type=F32)
        for h in range(2):
            for p in range((N + 2) // 2):
                at = 8 * p
                a = out[at : at + 8, h * X : (h + 1) * X]
                b = out[80 + at : 80 + at + 8, h * X : (h + 1) * X]
                c = out[160 + at : 160 + at + 8, h * X : (h + 1) * X]
                total = (
                    b
                    + jnp.where(first, 0.0, pltpu.roll(a, 1, 1))
                    + jnp.where(last, 0.0, pltpu.roll(c, X - 1, 1))
                )
                y = 2 * p - 1
                if y >= 0:
                    total = jnp.where(sublane == 3, spread_row(lab[plane + h, y : y + 1, :]), total)
                if y + 1 < N:
                    total = jnp.where(sublane == 7, spread_row(lab[plane + h, y + 1 : y + 2, :]), total)
                own[plane + h, at : at + 8, :] = total

    copies = []

    def send(src, dst, to):
        i = len(copies)
        copy = pltpu.make_async_remote_copy(
            src_ref=src, dst_ref=dst, send_sem=send_sem.at[i], recv_sem=recv_sem.at[i], device_id=to, device_id_type=MESH
        )
        copy.start()
        copies.append(copy)

    bottom, top = pl.ds(0, 16), pl.ds(ROWS - 16, 16)
    here = set()
    for chunk, pairs in enumerate(((0, 1, 2), (6, 7, 8), (3, 4, 5))):
        for z in FEATURE_ORDER:
            if z not in here and 2 * pairs[0] - 2 <= z <= 2 * pairs[-1] + 1:
                loads[z].wait()
                here.add(z)
        for j in pairs:
            two_planes(j)
        if chunk == 0:
            pl.semaphore_wait(barrier, count)
            send(row19, row19_in, (gz, y_dn))
        six = pl.ds(2 * pairs[0], 6)
        send(own.at[six, top, :], y_low.at[six], (gz, y_up))
        send(own.at[six, bottom, :], y_high.at[six], (gz, y_dn))
        if chunk == 0:
            send(own.at[pl.ds(0, 5)], z_high, (z_dn, yx))
            send(own.at[pl.ds(0, 4), top, :], high_low, (z_dn, y_up))
            send(own.at[pl.ds(0, 4), bottom, :], high_high, (z_dn, y_dn))
        if chunk == 1:
            send(own.at[pl.ds(N - 2, 4)], z_low, (z_up, yx))
            send(own.at[pl.ds(N - 2, 4), top, :], low_low, (z_up, y_up))
            send(own.at[pl.ds(N - 2, 4), bottom, :], low_high, (z_up, y_dn))

    has_zl, has_zh = (gz > 0).astype(F32), (gz < nz - 1).astype(F32)
    has_yl, has_yh = (yx > 0).astype(F32), (yx < ny - 1).astype(F32)
    kind = lax.rem(sublane, 4)
    bias = zero
    for o in range(3):
        bias = jnp.where(kind == o, jnp.broadcast_to(bias_v[0:1, o : o + 1], (8, X)), bias)
    keep_x = jnp.where((kind == 2) & last, 0.0, 1.0)
    is_label = kind == 3

    def plane_weights(plane, own_plane, zn, zn_plane, has_z, corner_low, corner_high, yn_plane, rows=range(11)):
        z = plane - LOW
        global_z = gz * N + z
        inside = jnp.logical_and(global_z >= 0, global_z < nz * N - 1).astype(F32)
        keep_zx = jnp.where(kind == 0, inside, keep_x)
        for v in rows:
            terms = []
            if 1 <= v <= 9:
                if own_plane is not None:
                    terms.append(own[own_plane, 8 * (v - 1) : 8 * v, :])
                if zn is not None:
                    terms.append(has_z * zn[zn_plane, 8 * (v - 1) : 8 * v, :])
            if v <= 1:
                if yn_plane is not None:
                    terms.append(has_yl * y_low[yn_plane, 8 * v : 8 * v + 8, :])
                if corner_low is not None:
                    terms.append((has_yl * has_z) * corner_low[zn_plane, 8 * v : 8 * v + 8, :])
            if v >= 9:
                if yn_plane is not None:
                    terms.append(has_yh * y_high[yn_plane, 8 * (v - 9) : 8 * (v - 9) + 8, :])
                if corner_high is not None:
                    terms.append((has_yh * has_z) * corner_high[zn_plane, 8 * (v - 9) : 8 * (v - 9) + 8, :])
            total = terms[0]
            for term in terms[1:]:
                total = total + term
            a = sigmoid(total + bias)
            raw[plane, 8 * v : 8 * v + 8, :] = jnp.where(is_label, (total == 0.0).astype(F32), a)
            mark[plane, 8 * v : 8 * v + 8, :] = total
            mark_right[plane, 8 * v : 8 * v + 8, :] = pltpu.roll(total, X - 1, 1)
            keep = keep_zx
            if v == 1:
                keep = jnp.where(sublane == 1, has_yl, keep)
            if v == 9:
                keep = jnp.where(sublane == 1, has_yh, keep)
            kept = a * keep
            before = pltpu.roll(jnp.where(is_label, total, kept), 1, 1)
            mark_left[plane, 8 * v : 8 * v + 8, :] = before
            edge[plane, 8 * v : 8 * v + 8, :] = jnp.where(is_label, pltpu.roll(before, 1, 0), kept)

    def middle(rows, group):
        def step(i, carry):
            for g in range(group):
                z = 1 + i * group + g
                plane_weights(z + LOW, z + 1, None, None, None, None, None, z + 1, rows)
            return carry

        lax.fori_loop(0, (N - 2) // group, step, 0)

    middle(range(2, 9), 14)
    for copy in copies:
        copy.wait()
    middle((0, 1, 9, 10), 14)
    for z in (-3, -2):
        plane_weights(z + LOW, None, z_low, z + 3, has_zl, low_low, low_high, None)
    for z in (-1, 0):
        plane_weights(z + LOW, z + 1, z_low, z + 3, has_zl, low_low, low_high, z + 1)
    for z in (15, 16):
        plane_weights(z + LOW, z + 1, z_high, z - 15, has_zh, high_low, high_high, z + 1)
    for z in (17, 18):
        plane_weights(z + LOW, None, z_high, z - 15, has_zh, high_low, high_high, None)

    def affinities_out(z, carry):
        for o in range(3):
            for h in range(2):
                at = pl.multiple_of(o * N * N + z * N + 8 * h, 8)
                aff_v[pl.ds(at, 8), :] = raw[z + LOW, pl.ds(4 * LOW + 32 * h + o, 8, stride=4), :]
        return carry

    lax.fori_loop(0, N, affinities_out, 0)
    stores = [pltpu.make_async_copy(aff_v, aff_ref, out_sem.at[0])]
    stores[-1].start()

    for z in range(N):
        mark[z + LOW, 4 * (EXT - 1) + 3 : 4 * EXT, :] = row19_in[z : z + 1, :]
    mark[EXT - 1, 8 : 8 + ROWS, :] = z_high[4]

    colour = (sublane + 1).astype(F32)

    def weight(plane, y, o):
        return spread_row(edge[plane, 4 * y + o : 4 * y + o + 1, :])

    def unseeded(plane, y):
        return spread_row(raw[plane, 4 * y + 3 : 4 * y + 4, :])

    def planes(body, low, high, group, carry):
        start, count = low + LOW, high - low + 1

        def step(i, carry):
            for g in range(group):
                carry = body(start + i * group + g, carry)
            return carry

        carry = lax.fori_loop(0, count // group, step, carry)
        for plane in range(start + count // group * group, start + count):
            carry = body(plane, carry)
        return carry

    def in_block(plane):
        return jnp.logical_and(plane >= LOW, plane < LOW + N).astype(F32)

    def first_step(plane, m0):
        plane_sum = zero
        before_w = weight(plane, 0, 1)
        for y in range(LOW - 2, LOW + N + 3):
            at = 4 * y + 3
            after_w = weight(plane, y, 1)
            total = zero
            for marks, where, w in (
                (mark, (plane - 1, at), weight(plane - 1, y, 0)),
                (mark, (plane + 1, at), weight(plane, y, 0)),
                (mark, (plane, at - 4), before_w),
                (mark, (plane, at + 4), after_w),
                (mark_left, (plane, at), weight(plane, y, 3)),
                (mark_right, (plane, at), weight(plane, y, 2)),
            ):
                label = spread_row(marks[where[0], where[1] : where[1] + 1, :])
                total = total - jnp.where(label == colour, w, 0.0)
            result = unseeded(plane, y) * total
            w0[plane, y] = result
            if LOW <= y < LOW + N:
                plane_sum = plane_sum + result * result
            before_w = after_w
        return m0 + in_block(plane) * plane_sum

    def store_block(i, w):
        inner = pl.ds(LOW, N)
        copy = pltpu.make_async_copy(w.at[inner, inner], basis_ref.at[i], out_sem.at[i + 1])
        copy.start()
        stores.append(copy)

    m0 = planes(first_step, -2, 18, 7, zero)
    store_block(0, w0)

    def apply(src, dst, low, high, group):
        rows = range(low + LOW, high + LOW + 1)
        y0 = rows[0]

        def step(plane, carry):
            below, crosses, squares = carry
            above = []
            here = src[plane, y0]
            flux_y_before = weight(plane, y0 - 1, 1) * (src[plane, y0 - 1] - here)
            cross = square = zero
            for y in rows:
                after = src[plane, y + 1]
                flux_z = weight(plane, y, 0) * (here - src[plane + 1, y])
                flux_y = weight(plane, y, 1) * (here - after)
                right = weight(plane, y, 2) * (here - pltpu.roll(here, X - 1, 1))
                left = weight(plane, y, 3) * (here - pltpu.roll(here, 1, 1))
                total = ((flux_z - below[y - y0]) + (flux_y - flux_y_before)) + (right + left)
                result = unseeded(plane, y) * total
                dst[plane, y] = result
                if LOW <= y < LOW + N:
                    cross = cross + here * result
                    square = square + result * result
                above.append(flux_z)
                here = after
                flux_y_before = flux_y
            mine = in_block(plane)
            return tuple(above), crosses + mine * cross, squares + mine * square

        start = low + LOW
        below = tuple(weight(start - 1, y, 0) * (src[start - 1, y] - src[start, y]) for y in rows)
        return planes(step, low, high, group, (below, zero, zero))[1:]

    m1, m2 = apply(w0, w1, -1, 17, 19)
    store_block(1, w1)
    m3, m4 = apply(w1, w2, 0, 16, 17)
    store_block(2, w2)

    def energy(plane, total):
        here = w2[plane, LOW]
        sums = zero
        for y in range(LOW, LOW + N):
            after = w2[plane, y + 1]
            d_z = here - w2[plane + 1, y]
            d_y = here - after
            d_x = here - pltpu.roll(here, X - 1, 1)
            sums = sums + (
                weight(plane, y, 0) * (d_z * d_z) + weight(plane, y, 1) * (d_y * d_y) + weight(plane, y, 2) * (d_x * d_x)
            )
            here = after
        return total + sums

    m5 = planes(energy, 0, N - 1, 8, zero)

    packed = zero
    for j, m in enumerate((m0, m1, m2, m3, m4, m5)):
        packed = jnp.where(lane == 8 * j + sublane, jnp.sum(m, axis=1, keepdims=True), packed)
    row = jnp.sum(packed, axis=0, keepdims=True)

    def all_sum(row, slots, me, count, stage, device):
        part[stage] = row
        slots[pl.ds(me, 1)] = row[None]
        copies = []
        for i in range(1, count):
            copy = pltpu.make_async_remote_copy(
                src_ref=part.at[stage], dst_ref=slots.at[me], send_sem=psend_sem.at[stage, i - 1],
                recv_sem=precv_sem.at[stage, i - 1], device_id=device(lax.rem(me + i, count)), device_id_type=MESH,
            )
            copy.start()
            copies.append(copy)
        for copy in copies:
            copy.wait()
        return jnp.sum(slots[...], axis=0)

    row = all_sum(row, sum_z, gz, nz, 0, lambda i: (i, yx))
    row = all_sum(row, sum_y, yx, ny, 1, lambda i: (gz, i))

    row = spread_row(row)
    mu = [
        jnp.broadcast_to(jnp.sum(jnp.where(lane == 8 * j + sublane, row, 0.0), axis=1, keepdims=True), (8, X))
        for j in range(6)
    ]

    def form(a, b, shift):
        total = None
        for i, p in enumerate(a):
            for j, q in enumerate(b):
                m = mu[i + j] if shift is None else mu[i + j + 1] + shift * mu[i + j]
                total = p * q * m if total is None else total + p * q * m
        return total

    one = jnp.ones((8, X), F32)
    residual, direction, answer = [one], [one], [zero] * ITERS
    rr = mu[0]
    for iteration in range(ITERS):
        length = jnp.clip(rr / form(direction, direction, RIDGE), STEP_LOW, STEP_HIGH)
        for i, d in enumerate(direction):
            answer[i] = answer[i] + length * d
        if iteration + 1 == ITERS:
            break
        shifted = [zero] + direction
        applied = [RIDGE * d + s for d, s in zip(direction + [zero], shifted)]
        residual = [r - length * a for r, a in zip(residual + [zero], applied)]
        after = form(residual, residual, None)
        beta = jnp.clip(after / rr, 0.0, BETA_HIGH)
        direction = [r + beta * d for r, d in zip(residual, direction + [zero])]
        rr = after

    for i in range(ITERS):
        answer_v[i] = answer[i]
    copy = pltpu.make_async_copy(answer_v, answer_ref, out_sem.at[4])
    copy.start()
    stores.append(copy)
    for copy in stores:
        copy.wait()


CHUNKS = 2
DEEP = N // CHUNKS


def finish_kernel(basis_ref, answer_ref, labels_ref, aff_in_ref, prob_ref, aff_ref, basis, answer, labels, prob, aff_v, in_sem, small_sem, out_sem):
    affinities = pltpu.make_async_copy(aff_in_ref, aff_v, small_sem.at[2])
    small = [
        pltpu.make_async_copy(answer_ref, answer, small_sem.at[0]),
        pltpu.make_async_copy(labels_ref, labels, small_sem.at[1]),
    ]
    for copy in small:
        copy.start()
    loads = []
    for j in range(CHUNKS):
        part = pl.ds(j * DEEP, DEEP)
        load = pltpu.make_async_copy(basis_ref.at[:, part], basis.at[:, part], in_sem.at[j])
        load.start()
        loads.append(load)
    affinities.start()
    for copy in small:
        copy.wait()
    colour = row_iota((8, X)) + 1
    a, b, c = (answer[i] for i in range(ITERS))
    stores = []
    for j in range(CHUNKS):
        loads[j].wait()

        def plane(z, carry):
            for y in range(N):
                seed = jnp.where(spread_row(labels[z, y : y + 1, :]) == colour, 1.0, 0.0)
                value = seed - (a * basis[0, z, y] + b * basis[1, z, y] + c * basis[2, z, y])
                prob[pl.ds(z * N + y, FIELDS, stride=N * N), :] = value
            return carry

        lax.fori_loop(j * DEEP, (j + 1) * DEEP, plane, 0)
        part = pl.ds(j * DEEP * N, DEEP * N)
        copy = pltpu.make_async_copy(prob.reshape(FIELDS, N * N, X).at[:, part], prob_ref.at[:, part], out_sem.at[j])
        copy.start()
        stores.append(copy)
        if j == 0:
            affinities.wait()
            affinities = pltpu.make_async_copy(aff_v, aff_ref, small_sem.at[2])
            affinities.start()
    stores.append(affinities)
    for copy in stores:
        copy.wait()


def body(features, conv_weight, conv_bias, labels):
    taps = conv_weight.transpose(0, 2, 3, 4, 1)
    vmem = pl.BlockSpec(memory_space=pltpu.VMEM)
    hbm = pl.BlockSpec(memory_space=pltpu.HBM)
    strips = [
        pltpu.VMEM((N + 2, 16, X), F32), pltpu.VMEM((N + 2, 16, X), F32),
        pltpu.VMEM((4, ROWS, X), F32), pltpu.VMEM((5, ROWS, X), F32),
        pltpu.VMEM((4, 16, X), F32), pltpu.VMEM((4, 16, X), F32),
        pltpu.VMEM((4, 16, X), F32), pltpu.VMEM((4, 16, X), F32),
        pltpu.VMEM((N, X), F32),
    ]
    basis, answer, aff = pl.pallas_call(
        kernel,
        out_shape=(
            jax.ShapeDtypeStruct((ITERS, N, N, FIELDS, X), F32),
            jax.ShapeDtypeStruct((ITERS, FIELDS, X), F32),
            jax.ShapeDtypeStruct((3 * N * N, X), F32),
        ),
        in_specs=[hbm] * 4,
        out_specs=(hbm,) * 3,
        scratch_shapes=[
            pltpu.VMEM((3, 3, 3, 3, CH), jnp.bfloat16),
            pltpu.VMEM((1, 3), F32),
            pltpu.VMEM((N + 4, CH, N, X), jnp.bfloat16),
            pltpu.VMEM((96, X), F32),
            pltpu.VMEM((96, CH * N), F32),
            pltpu.VMEM((240, 3 * CH * N), jnp.bfloat16),
            pltpu.VMEM((N, N, X), jnp.int32),
            pltpu.VMEM((N + 2, N, X), F32),
            pltpu.VMEM((N + 2, ROWS, X), F32),
            pltpu.VMEM((N, X), F32),
            *strips,
            pltpu.VMEM((EXT, 96, X), F32),
            pltpu.VMEM((EXT, 96, X), F32),
            pltpu.VMEM((EXT, 96, X), F32),
            pltpu.VMEM((EXT, 96, X), F32),
            pltpu.VMEM((EXT, 96, X), F32),
            pltpu.VMEM((EXT, EXT, 8, X), F32),
            pltpu.VMEM((EXT, EXT, 8, X), F32),
            pltpu.VMEM((EXT, EXT, 8, X), F32),
            pltpu.VMEM((2, 1, X), F32),
            pltpu.VMEM((8, 1, X), F32),
            pltpu.VMEM((32, 1, X), F32),
            pltpu.VMEM((3 * N * N, X), F32),
            pltpu.VMEM((ITERS, FIELDS, X), F32),
            pltpu.SemaphoreType.DMA((N,)),
            pltpu.SemaphoreType.DMA,
            pltpu.SemaphoreType.DMA((2,)),
            pltpu.SemaphoreType.DMA((5,)),
            pltpu.SemaphoreType.DMA((13,)),
            pltpu.SemaphoreType.DMA((13,)),
            pltpu.SemaphoreType.DMA((2, 31)),
            pltpu.SemaphoreType.DMA((2, 31)),
        ],
        compiler_params=pltpu.CompilerParams(collective_id=0, has_side_effects=True, vmem_limit_bytes=60 * 2**20),
    )(features, taps, conv_bias[None], labels)
    prob, aff = pl.pallas_call(
        finish_kernel,
        out_shape=(jax.ShapeDtypeStruct((FIELDS, N * N, X), F32), jax.ShapeDtypeStruct((3 * N * N, X), F32)),
        in_specs=[hbm] * 4,
        out_specs=(hbm, hbm),
        scratch_shapes=[
            pltpu.VMEM((ITERS, N, N, FIELDS, X), F32),
            pltpu.VMEM((ITERS, FIELDS, X), F32),
            pltpu.VMEM((N, N, X), jnp.int32),
            pltpu.VMEM((FIELDS * N * N, X), F32),
            pltpu.VMEM((3 * N * N, X), F32),
            pltpu.SemaphoreType.DMA((CHUNKS,)),
            pltpu.SemaphoreType.DMA((3,)),
            pltpu.SemaphoreType.DMA((CHUNKS,)),
        ],
        compiler_params=pltpu.CompilerParams(vmem_limit_bytes=60 * 2**20),
    )(basis, answer, labels, aff)
    return prob.reshape(FIELDS, N, N, X), aff.reshape(3, N, N, X)


def solution(mesh):
    in_specs = (P(None, "gz", "yx", None), P(), P(), P("gz", "yx", None))
    out_specs = (P(None, "gz", "yx", None), P(None, "gz", "yx", None))
    return jax.shard_map(body, mesh=mesh, in_specs=in_specs, out_specs=out_specs, check_vma=False)
```

```python
import jax
import jax.numpy as jnp
from jax import lax
from jax.experimental import pallas as pl
from jax.experimental.pallas import tpu as pltpu
from jax.sharding import PartitionSpec as P

FEATURE_ORDER = (*range(6), *range(10, 16), *range(6, 10))
MESH = pl.DeviceIdType.MESH
FIELDS = 8
ITERS = 3
RIDGE = 0.5
N = 16
X = 128
CH = 16
LOW = 3
EXT = N + 7
ROWS = 4 * (N + 2)
F32 = jnp.float32

STEP_LOW, STEP_HIGH = 1.0 / 12.5, 2.0
BETA_HIGH = 25.0


def lane_iota(shape):
    return lax.broadcasted_iota(jnp.int32, shape, len(shape) - 1)


def row_iota(shape):
    return lax.broadcasted_iota(jnp.int32, shape, len(shape) - 2)


def spread_row(row):
    return jnp.broadcast_to(row, (8, X))


def build_weights(conv_ref, rows_ref, taps_ref, lhs_ref):
    rows_ref[...] = jnp.zeros_like(rows_ref)
    for o in range(3):
        for dz in range(3):
            for dy in range(3):
                at = ((o * 3 + dz) * 3 + dy) * 3
                rows_ref[at : at + 3, 0:CH] = conv_ref[o, dz, dy].astype(F32)
    expand = (lax.div(lane_iota((X, CH * N)), N) == row_iota((X, CH * N))).astype(jnp.bfloat16)
    taps_ref[...] = jnp.dot(rows_ref[...].astype(jnp.bfloat16), expand, preferred_element_type=F32)
    columns = CH * N
    y_in = lax.rem(lane_iota((8, columns)), N)
    kind = lax.rem(row_iota((8, columns)), 4)
    half = lax.div(row_iota((8, columns)), 4)
    for dx in range(3):
        for dz in range(3):
            taps = []
            for dy in range(3):
                tap = jnp.zeros((8, columns), F32)
                for o in range(3):
                    at = ((o * 3 + dz) * 3 + dy) * 3 + dx
                    tap = jnp.where(kind == o, jnp.broadcast_to(taps_ref[at : at + 1, :], (8, columns)), tap)
                taps.append(tap)
            for pair in range(0, (N + 2) // 2, 2):
                blocks = []
                for p in (pair, pair + 1):
                    block = jnp.zeros((8, columns), F32)
                    if p < (N + 2) // 2:
                        gap = y_in - (2 * p - 1 + half) + 1
                        for dy in range(3):
                            block = jnp.where(gap == dy, taps[dy], block)
                    blocks.append(block)
                at = dx * 80 + pair * 8
                lhs_ref[at : at + 16, dz * columns : (dz + 1) * columns] = jnp.concatenate(blocks, axis=0).astype(jnp.bfloat16)


def sigmoid(x):
    e = jnp.exp(-jnp.abs(x))
    s = 1.0 / (1.0 + e)
    return jnp.where(x >= 0.0, s, e * s)


def kernel(
    feat_ref, conv_ref, bias_ref, labels_ref,
    basis_ref, answer_ref, aff_ref,
    conv, bias_v, feat, taps_rows, taps, lhs, labels, lab, own, row19,
    y_low, y_high, z_low, z_high, low_low, low_high, high_low, high_high, row19_in,
    raw, edge, mark, mark_left, mark_right, w0, w1, w2,
    part, sum_z, sum_y, aff_v, answer_v,
    feat_sem, label_sem, small_sem, out_sem, send_sem, recv_sem, psend_sem, precv_sem,
):
    gz, yx = lax.axis_index("gz"), lax.axis_index("yx")
    nz, ny = lax.axis_size("gz"), lax.axis_size("yx")
    z_up, z_dn = lax.rem(gz + 1, nz), lax.rem(gz + nz - 1, nz)
    y_up, y_dn = lax.rem(yx + 1, ny), lax.rem(yx + ny - 1, ny)

    barrier = pltpu.get_barrier_semaphore()
    count = 0
    for dz in (z_dn, gz, z_up):
        for dy in (y_dn, yx, y_up):
            if dz is gz and dy is yx:
                continue
            pl.semaphore_signal(barrier, inc=1, device_id=(dz, dy), device_id_type=MESH)
            count += 1
    for i in range(2, nz - 1):
        pl.semaphore_signal(barrier, inc=1, device_id=(lax.rem(gz + i, nz), yx), device_id_type=MESH)
        count += 1
    for i in range(2, ny - 1):
        pl.semaphore_signal(barrier, inc=1, device_id=(gz, lax.rem(yx + i, ny)), device_id_type=MESH)
        count += 1

    load_conv = pltpu.make_async_copy(conv_ref, conv, small_sem.at[0])
    load_bias = pltpu.make_async_copy(bias_ref, bias_v, small_sem.at[1])
    load_conv.start()
    load_bias.start()
    loads = [
        pltpu.make_async_copy(feat_ref.at[:, z], feat.at[z + 2], feat_sem.at[z])
        for z in range(N)
    ]
    load_labels = pltpu.make_async_copy(labels_ref, labels, label_sem)
    load_labels.start()
    for z in FEATURE_ORDER:
        loads[z].start()

    for p in (0, 1, N + 2, N + 3):
        feat[p] = jnp.zeros((CH, N, X), jnp.bfloat16)
    lab[0] = jnp.zeros((N, X), F32)
    lab[N + 1] = jnp.zeros((N, X), F32)
    load_conv.wait()
    load_bias.wait()
    build_weights(conv, taps_rows, taps, lhs)
    load_labels.wait()
    for z in range(N):
        lab[z + 1] = labels[z].astype(F32)
    for z in range(N):
        row19[z : z + 1, :] = lab[z + 1, 3:4, :]

    sublane = row_iota((8, X))
    lane = lane_iota((8, X))
    first, last = lane == 0, lane == X - 1
    zero = jnp.zeros((8, X), F32)

    def two_planes(j):
        plane = 2 * j
        left = feat[pl.ds(plane, 3)].reshape(3 * CH * N, X)
        right = feat[pl.ds(plane + 1, 3)].reshape(3 * CH * N, X)
        both = jnp.concatenate([left, right], axis=1)
        out = jnp.dot(lhs[...], both, preferred_element_type=F32)
        for h in range(2):
            for p in range((N + 2) // 2):
                at = 8 * p
                a = out[at : at + 8, h * X : (h + 1) * X]
                b = out[80 + at : 80 + at + 8, h * X : (h + 1) * X]
                c = out[160 + at : 160 + at + 8, h * X : (h + 1) * X]
                total = (
                    b
                    + jnp.where(first, 0.0, pltpu.roll(a, 1, 1))
                    + jnp.where(last, 0.0, pltpu.roll(c, X - 1, 1))
                )
                y = 2 * p - 1
                if y >= 0:
                    total = jnp.where(sublane == 3, spread_row(lab[plane + h, y : y + 1, :]), total)
                if y + 1 < N:
                    total = jnp.where(sublane == 7, spread_row(lab[plane + h, y + 1 : y + 2, :]), total)
                own[plane + h, at : at + 8, :] = total

    copies = []

    def send(src, dst, to):
        i = len(copies)
        copy = pltpu.make_async_remote_copy(
            src_ref=src, dst_ref=dst, send_sem=send_sem.at[i], recv_sem=recv_sem.at[i], device_id=to, device_id_type=MESH
        )
        copy.start()
        copies.append(copy)
        return copy

    row_copies = []
    bottom, top = pl.ds(0, 16), pl.ds(ROWS - 16, 16)
    here = set()
    for chunk, pairs in enumerate(((0, 1, 2), (6, 7, 8), (3, 4, 5))):
        for z in FEATURE_ORDER:
            if z not in here and 2 * pairs[0] - 2 <= z <= 2 * pairs[-1] + 1:
                loads[z].wait()
                here.add(z)
        for j in pairs:
            two_planes(j)
        if chunk == 0:
            pl.semaphore_wait(barrier, count)
            row_copies.append(send(row19, row19_in, (gz, y_dn)))
        six = pl.ds(2 * pairs[0], 6)
        row_copies.append(send(own.at[six, top, :], y_low.at[six], (gz, y_up)))
        row_copies.append(send(own.at[six, bottom, :], y_high.at[six], (gz, y_dn)))
        if chunk == 0:
            send(own.at[pl.ds(0, 5)], z_high, (z_dn, yx))
            send(own.at[pl.ds(0, 4), top, :], high_low, (z_dn, y_up))
            send(own.at[pl.ds(0, 4), bottom, :], high_high, (z_dn, y_dn))
        if chunk == 1:
            send(own.at[pl.ds(N - 2, 4)], z_low, (z_up, yx))
            send(own.at[pl.ds(N - 2, 4), top, :], low_low, (z_up, y_up))
            send(own.at[pl.ds(N - 2, 4), bottom, :], low_high, (z_up, y_dn))

    has_zl, has_zh = (gz > 0).astype(F32), (gz < nz - 1).astype(F32)
    has_yl, has_yh = (yx > 0).astype(F32), (yx < ny - 1).astype(F32)
    kind = lax.rem(sublane, 4)
    bias = zero
    for o in range(3):
        bias = jnp.where(kind == o, jnp.broadcast_to(bias_v[0:1, o : o + 1], (8, X)), bias)
    keep_x = jnp.where((kind == 2) & last, 0.0, 1.0)
    is_label = kind == 3

    def plane_weights(plane, own_plane, zn, zn_plane, has_z, corner_low, corner_high, yn_plane, rows=range(11)):
        z = plane - LOW
        global_z = gz * N + z
        inside = jnp.logical_and(global_z >= 0, global_z < nz * N - 1).astype(F32)
        keep_zx = jnp.where(kind == 0, inside, keep_x)
        for v in rows:
            terms = []
            if 1 <= v <= 9:
                if own_plane is not None:
                    terms.append(own[own_plane, 8 * (v - 1) : 8 * v, :])
                if zn is not None:
                    terms.append(has_z * zn[zn_plane, 8 * (v - 1) : 8 * v, :])
            if v <= 1:
                if yn_plane is not None:
                    terms.append(has_yl * y_low[yn_plane, 8 * v : 8 * v + 8, :])
                if corner_low is not None:
                    terms.append((has_yl * has_z) * corner_low[zn_plane, 8 * v : 8 * v + 8, :])
            if v >= 9:
                if yn_plane is not None:
                    terms.append(has_yh * y_high[yn_plane, 8 * (v - 9) : 8 * (v - 9) + 8, :])
                if corner_high is not None:
                    terms.append((has_yh * has_z) * corner_high[zn_plane, 8 * (v - 9) : 8 * (v - 9) + 8, :])
            total = terms[0]
            for term in terms[1:]:
                total = total + term
            a = sigmoid(total + bias)
            raw[plane, 8 * v : 8 * v + 8, :] = jnp.where(is_label, (total == 0.0).astype(F32), a)
            mark[plane, 8 * v : 8 * v + 8, :] = total
            mark_right[plane, 8 * v : 8 * v + 8, :] = pltpu.roll(total, X - 1, 1)
            keep = keep_zx
            if v == 1:
                keep = jnp.where(sublane == 1, has_yl, keep)
            if v == 9:
                keep = jnp.where(sublane == 1, has_yh, keep)
            kept = a * keep
            before = pltpu.roll(jnp.where(is_label, total, kept), 1, 1)
            mark_left[plane, 8 * v : 8 * v + 8, :] = before
            edge[plane, 8 * v : 8 * v + 8, :] = jnp.where(is_label, pltpu.roll(before, 1, 0), kept)

    def middle(rows, group):
        def step(i, carry):
            for g in range(group):
                z = 1 + i * group + g
                plane_weights(z + LOW, z + 1, None, None, None, None, None, z + 1, rows)
            return carry

        lax.fori_loop(0, (N - 2) // group, step, 0)

    colour = (sublane + 1).astype(F32)

    def weight(plane, y, o):
        return spread_row(edge[plane, 4 * y + o : 4 * y + o + 1, :])

    def unseeded(plane, y):
        return spread_row(raw[plane, 4 * y + 3 : 4 * y + 4, :])

    def planes(body, low, high, group, carry):
        start, count = low + LOW, high - low + 1

        def step(i, carry):
            for g in range(group):
                carry = body(start + i * group + g, carry)
            return carry

        carry = lax.fori_loop(0, count // group, step, carry)
        for plane in range(start + count // group * group, start + count):
            carry = body(plane, carry)
        return carry

    def in_block(plane):
        return jnp.logical_and(plane >= LOW, plane < LOW + N).astype(F32)

    def first_step(*runs):
        def step(plane, m0):
            plane_sum = zero
            for low, high in runs:
                before_w = weight(plane, low + LOW - 1, 1)
                for y in range(low + LOW, high + LOW + 1):
                    at = 4 * y + 3
                    after_w = weight(plane, y, 1)
                    total = zero
                    for marks, where, w in (
                        (mark, (plane - 1, at), weight(plane - 1, y, 0)),
                        (mark, (plane + 1, at), weight(plane, y, 0)),
                        (mark, (plane, at - 4), before_w),
                        (mark, (plane, at + 4), after_w),
                        (mark_left, (plane, at), weight(plane, y, 3)),
                        (mark_right, (plane, at), weight(plane, y, 2)),
                    ):
                        label = spread_row(marks[where[0], where[1] : where[1] + 1, :])
                        total = total - jnp.where(label == colour, w, 0.0)
                    result = unseeded(plane, y) * total
                    w0[plane, y] = result
                    if LOW <= y < LOW + N:
                        plane_sum = plane_sum + result * result
                    before_w = after_w
            return m0 + in_block(plane) * plane_sum

        return step

    middle(range(2, 9), 14)
    m0 = planes(first_step((2, 13)), 2, 13, 6, zero)
    for copy in row_copies:
        copy.wait()
    middle((0, 1, 9, 10), 14)
    for copy in copies:
        if all(copy is not done for done in row_copies):
            copy.wait()
    for z in (-3, -2):
        plane_weights(z + LOW, None, z_low, z + 3, has_zl, low_low, low_high, None)
    for z in (-1, 0):
        plane_weights(z + LOW, z + 1, z_low, z + 3, has_zl, low_low, low_high, z + 1)
    for z in (15, 16):
        plane_weights(z + LOW, z + 1, z_high, z - 15, has_zh, high_low, high_high, z + 1)
    for z in (17, 18):
        plane_weights(z + LOW, None, z_high, z - 15, has_zh, high_low, high_high, None)

    def affinities_out(z, carry):
        for o in range(3):
            for h in range(2):
                at = pl.multiple_of(o * N * N + z * N + 8 * h, 8)
                aff_v[pl.ds(at, 8), :] = raw[z + LOW, pl.ds(4 * LOW + 32 * h + o, 8, stride=4), :]
        return carry

    stores = [pltpu.make_async_copy(aff_v, aff_ref, out_sem.at[0])]

    for z in range(N):
        mark[z + LOW, 4 * (EXT - 1) + 3 : 4 * EXT, :] = row19_in[z : z + 1, :]
    mark[EXT - 1, 8 : 8 + ROWS, :] = z_high[4]

    def store_block(i, w):
        inner = pl.ds(LOW, N)
        copy = pltpu.make_async_copy(w.at[inner, inner], basis_ref.at[i], out_sem.at[i + 1])
        copy.start()
        stores.append(copy)

    m0 = planes(first_step((-2, 1), (14, 18)), 2, 13, 12, m0)
    m0 = planes(first_step((-2, 18)), -2, 1, 4, m0)
    m0 = planes(first_step((-2, 18)), 14, 18, 5, m0)
    store_block(0, w0)

    def apply(src, dst, low, high, group):
        rows = range(low + LOW, high + LOW + 1)
        y0 = rows[0]

        def step(plane, carry):
            below, crosses, squares = carry
            above = []
            here = src[plane, y0]
            flux_y_before = weight(plane, y0 - 1, 1) * (src[plane, y0 - 1] - here)
            cross = square = zero
            for y in rows:
                after = src[plane, y + 1]
                flux_z = weight(plane, y, 0) * (here - src[plane + 1, y])
                flux_y = weight(plane, y, 1) * (here - after)
                right = weight(plane, y, 2) * (here - pltpu.roll(here, X - 1, 1))
                left = weight(plane, y, 3) * (here - pltpu.roll(here, 1, 1))
                total = ((flux_z - below[y - y0]) + (flux_y - flux_y_before)) + (right + left)
                result = unseeded(plane, y) * total
                dst[plane, y] = result
                if LOW <= y < LOW + N:
                    cross = cross + here * result
                    square = square + result * result
                above.append(flux_z)
                here = after
                flux_y_before = flux_y
            mine = in_block(plane)
            return tuple(above), crosses + mine * cross, squares + mine * square

        start = low + LOW
        below = tuple(weight(start - 1, y, 0) * (src[start - 1, y] - src[start, y]) for y in rows)
        return planes(step, low, high, group, (below, zero, zero))[1:]

    m1, m2 = apply(w0, w1, -1, 17, 19)
    store_block(1, w1)
    m3, m4 = apply(w1, w2, 0, 16, 17)
    store_block(2, w2)

    def energy(plane, total):
        here = w2[plane, LOW]
        sums = zero
        for y in range(LOW, LOW + N):
            after = w2[plane, y + 1]
            d_z = here - w2[plane + 1, y]
            d_y = here - after
            d_x = here - pltpu.roll(here, X - 1, 1)
            sums = sums + (
                weight(plane, y, 0) * (d_z * d_z) + weight(plane, y, 1) * (d_y * d_y) + weight(plane, y, 2) * (d_x * d_x)
            )
            here = after
        return total + sums

    m5 = planes(energy, 0, N - 1, 8, zero)

    packed = zero
    for j, m in enumerate((m0, m1, m2, m3, m4, m5)):
        packed = jnp.where(lane == 8 * j + sublane, jnp.sum(m, axis=1, keepdims=True), packed)
    row = jnp.sum(packed, axis=0, keepdims=True)

    def all_sum(row, slots, me, count, stage, device, hops):
        part[stage] = row
        slots[pl.ds(me, 1)] = row[None]
        copies = []
        for i in sorted(range(1, count), key=hops, reverse=True):
            copy = pltpu.make_async_remote_copy(
                src_ref=part.at[stage], dst_ref=slots.at[me], send_sem=psend_sem.at[stage, i - 1],
                recv_sem=precv_sem.at[stage, i - 1], device_id=device(lax.rem(me + i, count)), device_id_type=MESH,
            )
            copy.start()
            copies.append(copy)
        if stage == 0:
            lax.fori_loop(0, N, affinities_out, 0)
            stores[0].start()
        for copy in copies:
            copy.wait()
        return jnp.sum(slots[...], axis=0)

    row = all_sum(row, sum_z, gz, nz, 0, lambda i: (i, yx), lambda i: min(i, nz - i))
    row = all_sum(row, sum_y, yx, ny, 1, lambda i: (gz, i), lambda i: min(i % 8, 8 - i % 8) + min(i // 8, 4 - i // 8))

    row = spread_row(row)
    mu = [
        jnp.broadcast_to(jnp.sum(jnp.where(lane == 8 * j + sublane, row, 0.0), axis=1, keepdims=True), (8, X))
        for j in range(6)
    ]

    def form(a, b, shift):
        total = None
        for i, p in enumerate(a):
            for j, q in enumerate(b):
                m = mu[i + j] if shift is None else mu[i + j + 1] + shift * mu[i + j]
                total = p * q * m if total is None else total + p * q * m
        return total

    one = jnp.ones((8, X), F32)
    residual, direction, answer = [one], [one], [zero] * ITERS
    rr = mu[0]
    for iteration in range(ITERS):
        length = jnp.clip(rr / form(direction, direction, RIDGE), STEP_LOW, STEP_HIGH)
        for i, d in enumerate(direction):
            answer[i] = answer[i] + length * d
        if iteration + 1 == ITERS:
            break
        shifted = [zero] + direction
        applied = [RIDGE * d + s for d, s in zip(direction + [zero], shifted)]
        residual = [r - length * a for r, a in zip(residual + [zero], applied)]
        after = form(residual, residual, None)
        beta = jnp.clip(after / rr, 0.0, BETA_HIGH)
        direction = [r + beta * d for r, d in zip(residual, direction + [zero])]
        rr = after

    for i in range(ITERS):
        answer_v[i] = answer[i]
    copy = pltpu.make_async_copy(answer_v, answer_ref, out_sem.at[4])
    copy.start()
    stores.append(copy)
    for copy in stores:
        copy.wait()


CHUNKS = 2
DEEP = N // CHUNKS


def finish_kernel(basis_ref, answer_ref, labels_ref, aff_in_ref, prob_ref, aff_ref, basis, answer, labels, prob, aff_v, in_sem, small_sem, out_sem):
    affinities = pltpu.make_async_copy(aff_in_ref, aff_v, small_sem.at[2])
    small = [
        pltpu.make_async_copy(answer_ref, answer, small_sem.at[0]),
        pltpu.make_async_copy(labels_ref, labels, small_sem.at[1]),
    ]
    for copy in small:
        copy.start()
    loads = []
    for j in range(CHUNKS):
        part = pl.ds(j * DEEP, DEEP)
        load = pltpu.make_async_copy(basis_ref.at[:, part], basis.at[:, part], in_sem.at[j])
        load.start()
        loads.append(load)
    affinities.start()
    for copy in small:
        copy.wait()
    colour = row_iota((8, X)) + 1
    a, b, c = (answer[i] for i in range(ITERS))
    stores = []
    for j in range(CHUNKS):
        loads[j].wait()

        def plane(z, carry):
            for y in range(N):
                seed = jnp.where(spread_row(labels[z, y : y + 1, :]) == colour, 1.0, 0.0)
                value = seed - (a * basis[0, z, y] + b * basis[1, z, y] + c * basis[2, z, y])
                prob[pl.ds(z * N + y, FIELDS, stride=N * N), :] = value
            return carry

        lax.fori_loop(j * DEEP, (j + 1) * DEEP, plane, 0)
        part = pl.ds(j * DEEP * N, DEEP * N)
        copy = pltpu.make_async_copy(prob.reshape(FIELDS, N * N, X).at[:, part], prob_ref.at[:, part], out_sem.at[j])
        copy.start()
        stores.append(copy)
        if j == 0:
            affinities.wait()
            affinities = pltpu.make_async_copy(aff_v, aff_ref, small_sem.at[2])
            affinities.start()
    stores.append(affinities)
    for copy in stores:
        copy.wait()


def body(features, conv_weight, conv_bias, labels):
    taps = conv_weight.transpose(0, 2, 3, 4, 1)
    vmem = pl.BlockSpec(memory_space=pltpu.VMEM)
    hbm = pl.BlockSpec(memory_space=pltpu.HBM)
    strips = [
        pltpu.VMEM((N + 2, 16, X), F32), pltpu.VMEM((N + 2, 16, X), F32),
        pltpu.VMEM((4, ROWS, X), F32), pltpu.VMEM((5, ROWS, X), F32),
        pltpu.VMEM((4, 16, X), F32), pltpu.VMEM((4, 16, X), F32),
        pltpu.VMEM((4, 16, X), F32), pltpu.VMEM((4, 16, X), F32),
        pltpu.VMEM((N, X), F32),
    ]
    basis, answer, aff = pl.pallas_call(
        kernel,
        out_shape=(
            jax.ShapeDtypeStruct((ITERS, N, N, FIELDS, X), F32),
            jax.ShapeDtypeStruct((ITERS, FIELDS, X), F32),
            jax.ShapeDtypeStruct((3 * N * N, X), F32),
        ),
        in_specs=[hbm] * 4,
        out_specs=(hbm,) * 3,
        scratch_shapes=[
            pltpu.VMEM((3, 3, 3, 3, CH), jnp.bfloat16),
            pltpu.VMEM((1, 3), F32),
            pltpu.VMEM((N + 4, CH, N, X), jnp.bfloat16),
            pltpu.VMEM((96, X), F32),
            pltpu.VMEM((96, CH * N), F32),
            pltpu.VMEM((240, 3 * CH * N), jnp.bfloat16),
            pltpu.VMEM((N, N, X), jnp.int32),
            pltpu.VMEM((N + 2, N, X), F32),
            pltpu.VMEM((N + 2, ROWS, X), F32),
            pltpu.VMEM((N, X), F32),
            *strips,
            pltpu.VMEM((EXT, 96, X), F32),
            pltpu.VMEM((EXT, 96, X), F32),
            pltpu.VMEM((EXT, 96, X), F32),
            pltpu.VMEM((EXT, 96, X), F32),
            pltpu.VMEM((EXT, 96, X), F32),
            pltpu.VMEM((EXT, EXT, 8, X), F32),
            pltpu.VMEM((EXT, EXT, 8, X), F32),
            pltpu.VMEM((EXT, EXT, 8, X), F32),
            pltpu.VMEM((2, 1, X), F32),
            pltpu.VMEM((8, 1, X), F32),
            pltpu.VMEM((32, 1, X), F32),
            pltpu.VMEM((3 * N * N, X), F32),
            pltpu.VMEM((ITERS, FIELDS, X), F32),
            pltpu.SemaphoreType.DMA((N,)),
            pltpu.SemaphoreType.DMA,
            pltpu.SemaphoreType.DMA((2,)),
            pltpu.SemaphoreType.DMA((5,)),
            pltpu.SemaphoreType.DMA((13,)),
            pltpu.SemaphoreType.DMA((13,)),
            pltpu.SemaphoreType.DMA((2, 31)),
            pltpu.SemaphoreType.DMA((2, 31)),
        ],
        compiler_params=pltpu.CompilerParams(collective_id=0, has_side_effects=True, vmem_limit_bytes=60 * 2**20),
    )(features, taps, conv_bias[None], labels)
    prob, aff = pl.pallas_call(
        finish_kernel,
        out_shape=(jax.ShapeDtypeStruct((FIELDS, N * N, X), F32), jax.ShapeDtypeStruct((3 * N * N, X), F32)),
        in_specs=[hbm] * 4,
        out_specs=(hbm, hbm),
        scratch_shapes=[
            pltpu.VMEM((ITERS, N, N, FIELDS, X), F32),
            pltpu.VMEM((ITERS, FIELDS, X), F32),
            pltpu.VMEM((N, N, X), jnp.int32),
            pltpu.VMEM((FIELDS * N * N, X), F32),
            pltpu.VMEM((3 * N * N, X), F32),
            pltpu.SemaphoreType.DMA((CHUNKS,)),
            pltpu.SemaphoreType.DMA((3,)),
            pltpu.SemaphoreType.DMA((CHUNKS,)),
        ],
        compiler_params=pltpu.CompilerParams(vmem_limit_bytes=60 * 2**20),
    )(basis, answer, labels, aff)
    return prob.reshape(FIELDS, N, N, X), aff.reshape(3, N, N, X)


def solution(mesh):
    in_specs = (P(None, "gz", "yx", None), P(), P(), P("gz", "yx", None))
    out_specs = (P(None, "gz", "yx", None), P(None, "gz", "yx", None))
    return jax.shard_map(body, mesh=mesh, in_specs=in_specs, out_specs=out_specs, check_vma=False)
```
